256 devices in a mesh: dp: 16 (over z_hi, y), fsdp: 16 (over x, z_lo, core).
Axes of the slice: x: 4, y: 4, z: 8 (z_hi: 4, z_lo: 2; z = z_hi * 2 + z_lo), core: 2. Of those that a mesh axis runs over, the one named last changes fastest.
Arguments:
- tokens: bfloat16 [512, 256, 768], P(('dp', 'fsdp')), may hold values from -30 to 30
- cotangent: bfloat16 [512, 256, 768], P(('dp', 'fsdp')), may hold values from -6 to 6
- live_index: int32 [512, 256], P(('dp', 'fsdp')), may hold values from 0 to 255, as said below
- live_count: int32 [512], P(('dp', 'fsdp')), may hold values from 1 to 256, as said below
- norm_gain: bfloat16 [768], P('fsdp'), may hold values from 0.099609375 to 1.8984375
- w_first: bfloat16 [768, 3072], P('fsdp'), may hold values from -0.21875 to 0.21875
- w_second: bfloat16 [3072, 768], P('fsdp'), may hold values from -0.109375 to 0.109375
Outputs:
- layer_out: bfloat16 [512, 256, 768], P(('dp', 'fsdp'))
- token_grad: bfloat16 [512, 256, 768], P(('dp', 'fsdp'))
- grad_first: float32 [768, 3072], P('fsdp')
- grad_second: float32 [3072, 768], P('fsdp')
- grad_gain: float32 [768], P('fsdp')
The draws below stay inside these ranges and needn't reach their ends.
Inputs may be any that keep to these rules, and one draw needn't show every extreme that they name: `live_index`: row i names each of the 256 patches once; its first live_count[i] entries are the live patches, ascending. `live_count`: images are laid out 2 to a device. For two devices with the same fsdp index whose dp indices differ by 8, round each device's number of live patches (over its 2 images) up to a multiple of 128; the two rounded numbers add up to at most 768 = 768.
All inputs are finite; a program needn't handle non-finite values.
Results may differ from the reference program's by a relative error of at most 0.0055.
Values may be sent and summed in bfloat16 or wider, within the bound.
A program may use at most 128 MiB of HBM per device.

```python
import math
import jax
import jax.numpy as jnp
from jax import lax

D = 768
H = 3072
P_SIZE = 256
IMG_DEV = 2
IMAGES = 512
N_DP = 16
N_FSDP = 16


def live_totals(key):
    rows_dev = IMG_DEV * P_SIZE
    half = N_DP // 2
    pairs = half * N_FSDP
    devices = N_DP * N_FSDP
    keys = jax.random.split(key, 6)
    kinds = jax.random.randint(keys[0], (pairs,), 0, 4).at[0].set(0)
    sides = jax.random.randint(keys[1], (pairs,), 0, 2)
    heavy = jax.random.randint(keys[2], (pairs,), rows_dev - 127, rows_dev + 1).at[0].set(rows_dev)
    light = jax.random.randint(keys[3], (pairs,), IMG_DEV, rows_dev - 255)
    evened = jax.random.randint(keys[4], (2, pairs), IMG_DEV, rows_dev - 127)
    lower = jnp.where(kinds < 3, jnp.where(sides == 0, heavy, light), evened[0])
    upper = jnp.where(kinds < 3, jnp.where(sides == 0, light, heavy), evened[1])
    totals = jnp.concatenate([lower.reshape(half, N_FSDP), upper.reshape(half, N_FSDP)], axis=0).reshape(-1)
    base = totals // IMG_DEV
    extra = totals % IMG_DEV
    order = jnp.arange(IMG_DEV, dtype=jnp.int32)
    counts = base[:, None] + (order[None, :] < extra[:, None]).astype(jnp.int32)
    for first in range(0, IMG_DEV - 1, 2):
        former = counts[:, first]
        latter = counts[:, first + 1]
        room = jnp.minimum(jnp.minimum(former - 1, P_SIZE - former), jnp.minimum(latter - 1, P_SIZE - latter))
        moved = jax.random.randint(jax.random.fold_in(keys[5], first), (devices,), -room, room + 1)
        counts = counts.at[:, first].add(moved).at[:, first + 1].add(-moved)
    return counts.reshape(-1).astype(jnp.int32)


def draw_live_count(key, part):
    return live_totals(key)


def draw_live_index(key, part):
    counts = live_totals(key)
    key = jax.random.fold_in(key, 5)
    shuffled = jax.vmap(lambda single: jax.random.permutation(single, P_SIZE))(jax.random.split(key, IMAGES))
    ranks = jnp.argsort(shuffled, axis=1).astype(jnp.int32)
    patch_ids = jnp.arange(P_SIZE, dtype=jnp.int32)[None, :]
    scores = jnp.where(ranks < counts[:, None], patch_ids, P_SIZE + patch_ids)
    return jnp.argsort(scores, axis=1).astype(jnp.int32)


def draw_tokens(key, part):
    key = jax.random.fold_in(key, 11)
    keys = jax.random.split(key, 3)
    column = jnp.exp(jax.random.uniform(keys[0], (D,), minval=math.log(0.3), maxval=math.log(3.0)))
    row_scale = jnp.exp(jax.random.uniform(keys[1], (IMAGES, P_SIZE, 1), minval=math.log(0.5), maxval=math.log(2.0)))
    values = jax.random.normal(keys[2], (IMAGES, P_SIZE, D))
    return jnp.clip(values * column * row_scale, -30.0, 30.0).astype(jnp.bfloat16)


def block_levels(own_key, dims, cuts, least, largest):
    def one(dim, shards_of):
        draws = jax.random.uniform(jax.random.fold_in(jax.random.fold_in(own_key, 6), dim), (shards_of,), jnp.float32, least / len(cuts), largest / len(cuts))
        return jnp.repeat(jnp.exp(draws), dims[dim] // shards_of).reshape((-1,) + (1,) * (len(dims) - dim - 1))

    loudness = one(*cuts[0])
    for cut in cuts[1:]:
        loudness = loudness * one(*cut)
    return loudness


def noise(key, extent, scale, reach, shards=(), kind=jnp.bfloat16):
    factor_of = block_levels(key, extent, shards, -0.22, 0.18) if shards else 1.0
    result = jax.random.normal(key, extent, jnp.float32) * scale * factor_of
    return jnp.minimum(jnp.maximum(result, -reach), reach).astype(kind)


def setup_inputs(seed: int = 0) -> dict:
    streams_of = jax.random.split(jax.random.key(seed), 8)
    return {
        "tokens": draw_tokens(jax.random.fold_in(streams_of[7], 71), 0),
        "cotangent": noise(streams_of[1], (IMAGES, P_SIZE, D), 1.0, 6.0, ((0, 256),)),
        "live_index": draw_live_index(jax.random.fold_in(streams_of[7], 71), 0),
        "live_count": draw_live_count(jax.random.fold_in(streams_of[7], 71), 0),
        "norm_gain": jnp.clip(1.0 + 0.18 * jax.random.normal(streams_of[4], (D,), jnp.float32), 0.099609375, 1.8984375).astype(jnp.bfloat16),
        "w_first": noise(streams_of[5], (D, H), D ** -0.5, 0.21875, ((0, 16),)),
        "w_second": noise(streams_of[6], (H, D), H ** -0.5, 0.109375, ((0, 16),)),
    }


epsilon = 1e-06
root_two_pi = 0.7978845608028654
cubic = 0.044715

def gelu_value(before):
    inner = root_two_pi * (before + cubic * before * before * before)
    return 0.5 * before * (1.0 + jnp.tanh(inner))

def gelu_slope(before):
    inner = root_two_pi * (before + cubic * before * before * before)
    tangent = jnp.tanh(inner)
    return 0.5 * (1.0 + tangent) + 0.5 * before * (1.0 - tangent * tangent) * root_two_pi * (1.0 + 3.0 * cubic * before * before)

def live_rows(live_index, live_count):
    images, patches = live_index.shape
    order = jnp.arange(patches, dtype=jnp.int32)
    marks = (order[None, :] < live_count[:, None]).astype(jnp.int32)
    owners = jnp.broadcast_to(jnp.arange(images, dtype=jnp.int32)[:, None], (images, patches))
    return jnp.zeros((images, patches), jnp.int32).at[owners, live_index].set(marks) > 0

def layer_pass(token_rows, upstream, gain_full, first_full, second_full):
    values = token_rows.astype(jnp.float32)
    center = lax.optimization_barrier(jnp.mean(values, axis=1, keepdims=True))
    spread = lax.optimization_barrier(jnp.mean(jnp.square(values - center), axis=1, keepdims=True))
    inverse = lax.rsqrt(spread + epsilon)
    normed = (values - center) * inverse
    gain_value = gain_full.astype(jnp.float32)
    normal_rows = (normed * gain_value).astype(jnp.bfloat16)
    before = jnp.dot(normal_rows, first_full, preferred_element_type=jnp.float32)
    hidden = gelu_value(before).astype(jnp.bfloat16)
    mixed_rows = (values + jnp.dot(hidden, second_full, preferred_element_type=jnp.float32)).astype(jnp.bfloat16)
    back_hidden = lax.dot_general(upstream, second_full, (((1,), (1,)), ((), ())), preferred_element_type=jnp.float32)
    back_before = (back_hidden * gelu_slope(before)).astype(jnp.bfloat16)
    back_normal = lax.dot_general(back_before, first_full, (((1,), (1,)), ((), ())), preferred_element_type=jnp.float32)
    gain_term = lax.optimization_barrier(jnp.sum(back_normal * normed, axis=0))
    scaled_back = back_normal * gain_value
    grad_rows = upstream.astype(jnp.float32) + inverse * (scaled_back - lax.optimization_barrier(jnp.mean(scaled_back, axis=1, keepdims=True)) - normed * lax.optimization_barrier(jnp.mean(scaled_back * normed, axis=1, keepdims=True)))
    return (mixed_rows, grad_rows.astype(jnp.bfloat16), gain_term, normal_rows, hidden, back_before)

def reference(tokens, cotangent, live_index, live_count, norm_gain, w_first, w_second):
    images, patches, width = tokens.shape
    hidden_width = w_first.shape[1]
    live_flag = live_rows(live_index, live_count)
    group = IMG_DEV
    blocks = images // group
    scale = 1.0 / patches

    def advance(carry, inputs):
        token_block, upstream_block, flag_block = inputs
        flag_column = flag_block.reshape(-1, 1)
        work_tokens = jnp.where(flag_column, token_block, jnp.zeros_like(token_block))
        work_upstream = jnp.where(flag_column, upstream_block, jnp.zeros_like(upstream_block))
        outcome = layer_pass(work_tokens, work_upstream, norm_gain, w_first, w_second)
        first_term = lax.dot_general(outcome[3], outcome[5], (((0,), (0,)), ((), ())), preferred_element_type=jnp.float32)
        second_term = lax.dot_general(outcome[4], work_upstream, (((0,), (0,)), ((), ())), preferred_element_type=jnp.float32)
        carry = (carry[0] + outcome[2] * scale, carry[1] + first_term * scale, carry[2] + second_term * scale)
        layer_block = jnp.where(flag_column, outcome[0], token_block)
        grad_block = jnp.where(flag_column, outcome[1], upstream_block)
        return (carry, (layer_block, grad_block))
    init = (jnp.zeros((width,), jnp.float32), jnp.zeros((width, hidden_width), jnp.float32), jnp.zeros((hidden_width, width), jnp.float32))
    inputs = (tokens.reshape(blocks, group * patches, width), cotangent.reshape(blocks, group * patches, width), live_flag.reshape(blocks, group * patches))
    totals, outputs = lax.scan(advance, init, inputs)
    layer_out = outputs[0].reshape(images, patches, width)
    token_grad = outputs[1].reshape(images, patches, width)
    return (layer_out, token_grad, totals[1], totals[2], totals[0])
```

```python
import functools

import jax
import jax.numpy as jnp
from jax import lax
from jax.experimental import pallas as pl
from jax.experimental.pallas import tpu as pltpu
from jax.sharding import PartitionSpec as P

epsilon = 1e-06
root_two_pi = 0.7978845608028654
cubic = 0.044715

MESH = pl.DeviceIdType.MESH
NX, NY, NZH = 4, 4, 4
D, H, ROWS, PATCHES = 768, 3072, 512, 256
C = 6
HS = 192 // C
CW = 8 * HS
R1, R2 = D // 8, D * HS // CW
NB = D // CW
SR = R1 + R2
PR = SR // NY
SCALE = 1.0 / PATCHES
F32, BF16 = jnp.float32, jnp.bfloat16


def rem(a, n):
    return lax.rem(a, jnp.int32(n))


def kernel(tok, cot, idx, cnt, gain, w1, w2, o_out, o_grad, o_g1, o_g2, o_gain,
           wg, tk, ct, nrm, nt, nf, inv_s, flag_s, hid, bb, buf, r1, s1, r2, s2, r3, r4, fin, gx,
           po, pb, px, rx, gt, gsum, gz, gxx, gyy, gzz,
           ag_s, ag_r, q1_s, q1_r, q2_s, q2_r, q3_s, q3_r, q4_s, q4_r, q5_s, q5_r, q6_s, q6_r,
           w_s, w_r, l_s, t_s, t_r, gg_s, gg_r, p_s, p_r, a_s, a_r):
    dp, f = lax.axis_index("dp"), lax.axis_index("fsdp")
    x, zl, k = lax.div(f, jnp.int32(4)), rem(lax.div(f, jnp.int32(2)), 2), rem(f, 2)
    zh, y = lax.div(dp, jnp.int32(4)), rem(dp, 4)
    z, q = zh * 2 + zl, lax.div(f, jnp.int32(2))

    def dev(x_, y_, z_, k_):
        return (lax.div(z_, jnp.int32(2)) * 4 + y_, x_ * 4 + rem(z_, 2) * 2 + k_)

    z_near = zh * 2 + (1 - zl)
    z_far = rem(z + 8 + 2 * zl - 1, 8)
    partner = dev(x, y, z, 1 - k)
    near, far = dev(x, y, z_near, k), dev(x, y, z_far, k)
    xp = [dev(rem(x + i, NX), y, z, k) for i in range(1, NX)]
    yp = [dev(x, rem(y + i, NY), z, k) for i in range(1, NY)]
    zp = [dev(x, y, rem(z + 2 * i, 8), k) for i in range(1, NZH)]

    def send(src, dst, s_sem, r_sem, to):
        copy = pltpu.make_async_remote_copy(
            src_ref=src, dst_ref=dst, send_sem=s_sem, recv_sem=r_sem, device_id=to, device_id_type=MESH
        )
        copy.start()

    def got(ref, sem):
        pltpu.make_async_copy(ref, ref, sem).wait()

    everyone = [partner, near, far] + xp + yp + zp
    barrier = pltpu.get_barrier_semaphore()
    for peer in everyone:
        pl.semaphore_signal(barrier, inc=1, device_id=peer, device_id_type=MESH)
    pl.semaphore_wait(barrier, len(everyone))

    mine = pl.ds(pl.multiple_of(R1 // 2 * k, 16), R1 // 2)
    other = pl.ds(pl.multiple_of(R1 // 2 * (1 - k), 16), R1 // 2)
    send(w1.at[1 - k], wg.at[:, q, mine, :], w_s, w_r, partner)
    own = pltpu.make_async_copy(w1.at[k], wg.at[:, q, mine, :], l_s)
    own.start()
    g_own = gain[...]
    g_own = jnp.where(k == 1, pltpu.roll(g_own, 48, 1), g_own)
    gsum[0] = g_own
    send(gsum.at[0], gsum.at[1], gg_s.at[0], gg_r.at[0], partner)
    for c in range(C):
        for n in range(NB):
            wg[c, q, R1 + HS * n : R1 + HS * (n + 1), :] = w2[HS * c : HS * (c + 1), CW * n : CW * (n + 1)]
    own.wait()
    got(wg.at[:, q, other, :], w_r)

    def first_sends(c, carry):
        for i in range(1, NX):
            send(wg.at[c, q], wg.at[c, q], ag_s.at[c, i - 1], ag_r.at[c, i - 1], xp[i - 1])
        to = tuple(jnp.where(x < 2, a, b) for a, b in zip(near, far))
        send(wg.at[c, q], wg.at[c, q], ag_s.at[c, 3], ag_r.at[c, 3 + x], to)
        return carry

    lax.fori_loop(0, C, first_sends, 0)

    got(gsum.at[1], gg_r.at[0])
    gt[zl, x] = gsum[0] + gsum[1]
    for i in range(1, NX):
        send(gt.at[zl, x], gt.at[zl, x], gg_s.at[i], gg_r.at[i], xp[i - 1])

    for image in range(2):
        at = lax.broadcasted_iota(jnp.int32, (PATCHES, PATCHES), 0)
        place = lax.broadcasted_iota(jnp.int32, (PATCHES, PATCHES), 1)
        hit = jnp.where(
            jnp.logical_and(idx[image : image + 1, :] == at, place < cnt[image]), 1.0, 0.0
        ).astype(F32)
        flag = jnp.max(hit, axis=1, keepdims=True)
        rows = slice(PATCHES * image, PATCHES * (image + 1))
        flag_s[rows, :] = jnp.broadcast_to(flag, (PATCHES, 128))
        to = pl.ds(pl.multiple_of(ROWS * k + PATCHES * image, PATCHES), PATCHES)
        tk[to, :] = jnp.where(flag > 0, tok[rows, :].astype(F32), 0.0).astype(BF16)
        ct[to, :] = jnp.where(flag > 0, cot[rows, :].astype(F32), 0.0).astype(BF16)
    here = pl.ds(pl.multiple_of(ROWS * k, ROWS), ROWS)
    there = pl.ds(pl.multiple_of(ROWS * (1 - k), ROWS), ROWS)
    send(tk.at[here], tk.at[here], t_s.at[0], t_r.at[0], partner)
    send(ct.at[here], ct.at[here], t_s.at[1], t_r.at[1], partner)

    def forward(c):
        for i in range(1, NX):
            xs = rem(x + NX - i, NX)
            qs = xs * 2 + zl
            got(wg.at[c, qs], ag_r.at[c, i - 1])
            to = tuple(jnp.where(xs < 2, a, b) for a, b in zip(near, far))
            send(wg.at[c, qs], wg.at[c, qs], ag_s.at[c, 3 + i], ag_r.at[c, 3 + xs], to)

    for i in range(1, NX):
        got(gt.at[zl, rem(x + NX - i, NX)], gg_r.at[i])
    send(gt.at[zl], gt.at[zl], gg_s.at[4], gg_r.at[4], near)
    forward(0)
    got(gt.at[1 - zl], gg_r.at[4])
    got(tk.at[there], t_r.at[0])
    got(ct.at[there], t_r.at[1])

    def gain_row():
        total = jnp.zeros((8, D), F32)
        for qs in range(8):
            tile = jnp.concatenate([gt[qs % 2, qs // 2], jnp.zeros((8, D - 128), F32)], axis=1)
            total = total + (pltpu.roll(tile, 96 * qs, 1) if qs else tile)
        return total[0:1, :]

    gains = gain_row()

    def norm_step(m, carry):
        rows = pl.ds(pl.multiple_of(256 * m, 256), 256)
        values = tk[rows, :].astype(F32)
        center = jnp.mean(values, axis=1, keepdims=True)
        values = values - center
        spread = jnp.mean(values * values, axis=1, keepdims=True)
        inverse = lax.rsqrt(spread + epsilon)
        normed = values * inverse
        nf[rows, :] = normed
        inv_s[rows, :] = jnp.broadcast_to(inverse, (256, 128))
        normal = normed * gains
        nrm[rows, :] = normal.astype(BF16)
        nt[:, rows] = jnp.transpose(normal).astype(BF16)
        return carry

    lax.fori_loop(0, 4, norm_step, 0)

    def first_of(c):
        return wg[c, :, 0:R1, :].reshape(D, CW)

    def second_of(c, n):
        return wg[c, :, R1 + HS * n : R1 + HS * (n + 1), :].reshape(CW, CW)

    def grads(c):
        for i in range(4):
            qs = 2 * i + 1 - zl
            got(wg.at[c, qs], ag_r.at[c, 3 + i])

        def step(m, carry):
            rows = pl.ds(pl.multiple_of(256 * m, 256), 256)
            before = jnp.dot(nrm[rows, :], first_of(c), preferred_element_type=F32)
            back = jnp.zeros((256, CW), F32)
            for n in range(NB):
                back = back + lax.dot_general(
                    ct[rows, CW * n : CW * (n + 1)], second_of(c, n), (((1,), (1,)), ((), ())),
                    preferred_element_type=F32,
                )
            square = before * before
            tangent = jnp.tanh(before * (root_two_pi + (root_two_pi * cubic) * square))
            half = 0.5 + 0.5 * tangent
            hid[c, rows, :] = (before * half).astype(BF16)
            slope = half + (0.5 * before) * (1.0 - tangent * tangent) * (
                root_two_pi + (3.0 * cubic * root_two_pi) * square
            )
            bb[c, rows, :] = (back * slope).astype(BF16)
            return carry

        lax.fori_loop(0, 4, step, 0)
        for part in range(2):
            term = jnp.dot(nt[384 * part : 384 * (part + 1), :], bb[c], preferred_element_type=F32)
            term = (term * SCALE).astype(BF16)
            for i in range(4):
                qs = 4 * part + i
                buf[c, qs % 2, qs // 2, 0:R1, :] = term[R1 * i : R1 * (i + 1), :]
        for n in range(NB):
            term = lax.dot_general(
                hid[c], ct[:, CW * n : CW * (n + 1)], (((0,), (0,)), ((), ())), preferred_element_type=F32
            )
            term = (term * SCALE).astype(BF16)
            for qs in range(8):
                buf[c, qs % 2, qs // 2, R1 + HS * n : R1 + HS * (n + 1), :] = term[HS * qs : HS * (qs + 1), :]
        send(buf.at[c, 1 - zl, 0:2], r1.at[c, 0:2], q1_s.at[c, 0], q1_r.at[c, 0], near)
        send(buf.at[c, 1 - zl, 2:4], r1.at[c, 2:4], q1_s.at[c, 1], q1_r.at[c, 1], far)

    def along_z_lo(c):
        got(r1.at[c, 0:2], q1_r.at[c, 0])
        got(r1.at[c, 2:4], q1_r.at[c, 1])
        for i in range(NX):
            s1[c, i] = (buf[c, zl, i].astype(F32) + r1[c, i].astype(F32)).astype(BF16)
        for i in range(1, NX):
            send(s1.at[c, rem(x + i, NX)], r2.at[c, i - 1], q2_s.at[c, i - 1], q2_r.at[c, i - 1], xp[i - 1])

    def along_x(c):
        for i in range(NX - 1):
            got(r2.at[c, i], q2_r.at[c, i])
        total = s1[c, x].astype(F32)
        for i in range(NX - 1):
            total = total + r2[c, i].astype(F32)
        s2[c] = total.astype(BF16)
        for i in range(1, NY):
            part = pl.ds(pl.multiple_of(PR * rem(y + i, NY), 16), PR)
            send(s2.at[c, part], r3.at[c, i - 1], q3_s.at[c, i - 1], q3_r.at[c, i - 1], yp[i - 1])

    def along_y(c):
        for i in range(NY - 1):
            got(r3.at[c, i], q3_r.at[c, i])
        total = s2[c, pl.ds(pl.multiple_of(PR * y, 16), PR), :].astype(F32)
        for i in range(NY - 1):
            total = total + r3[c, i].astype(F32)
        r4[c, zh] = total.astype(BF16)
        for i in range(1, NZH):
            send(r4.at[c, zh], r4.at[c, zh], q4_s.at[c, i - 1], q4_r.at[c, i - 1], zp[i - 1])

    def along_z_hi(c):
        for i in range(1, NZH):
            got(r4.at[c, rem(zh + NZH - i, NZH)], q4_r.at[c, i - 1])
        total = r4[c, 0].astype(F32)
        for i in range(1, NZH):
            total = total + r4[c, i].astype(F32)
        fin[c, y] = total.astype(BF16)
        for i in range(1, NY):
            send(fin.at[c, y], fin.at[c, y], q5_s.at[c, i - 1], q5_r.at[c, i - 1], yp[i - 1])

    def back_y(c):
        for i in range(1, NY):
            got(fin.at[c, rem(y + NY - i, NY)], q5_r.at[c, i - 1])
        send(fin.at[c, 1 - k], gx.at[c], q6_s.at[c], q6_r.at[c], partner)
        o_g1[k, c] = fin[c, k]
        second = fin[c, 2:4].reshape(R2, CW)
        rows = pl.ds(pl.multiple_of(HS * c, HS), HS)
        for n in range(NB):
            o_g2[rows, CW * n : CW * (n + 1)] = second[HS * n : HS * (n + 1), :]

    def out_rows(start):
        rows = pl.ds(pl.multiple_of(start, 256), 256)
        parts = []
        for n in range(NB):
            total = jnp.zeros((256, CW), F32)
            for c in range(C):
                total = total + jnp.dot(hid[c, rows, :], second_of(c, n), preferred_element_type=F32)
            parts.append(total)
        return parts

    def back_rows(start):
        rows = pl.ds(pl.multiple_of(start, 256), 256)
        total = jnp.zeros((256, D), F32)
        for c in range(C):
            total = total + lax.dot_general(
                bb[c, rows, :], first_of(c), (((1,), (1,)), ((), ())), preferred_element_type=F32
            )
        return total

    def tail_out():
        def step(m, carry):
            rows = pl.ds(pl.multiple_of(256 * m, 256), 256)
            for n, part in enumerate(out_rows(ROWS * (1 - k) + 256 * m)):
                px[0, rows, CW * n : CW * (n + 1)] = part.astype(BF16)
            px[1, rows, :] = back_rows(ROWS * (1 - k) + 256 * m).astype(BF16)
            return carry

        lax.fori_loop(0, 2, step, 0)
        for i in range(2):
            send(px.at[i], rx.at[i], p_s.at[i], p_r.at[i], partner)

        def step(m, carry):
            rows = pl.ds(pl.multiple_of(256 * m, 256), 256)
            for n, part in enumerate(out_rows(ROWS * k + 256 * m)):
                po[rows, CW * n : CW * (n + 1)] = part
            pb[rows, :] = back_rows(ROWS * k + 256 * m)
            return carry

        lax.fori_loop(0, 2, step, 0)

    def tail_rows():
        for i in range(2):
            got(rx.at[i], p_r.at[i])
        gsum[2] = jnp.zeros((8, 128), F32)
        gsum[3] = jnp.zeros((8, 128), F32)

        def step(m, term):
            rows = pl.ds(pl.multiple_of(128 * m, 128), 128)
            at = pl.ds(pl.multiple_of(ROWS * k + 128 * m, 128), 128)
            live = flag_s[rows, :][:, 0:1] > 0
            plain = tok[rows, :].astype(F32)
            mixed = plain + (po[rows, :] + rx[0, rows, :].astype(F32))
            o_out[rows, :] = jnp.where(live, mixed, plain).astype(BF16)
            normed = nf[at, :]
            inverse = inv_s[at, :][:, 0:1]
            back = pb[rows, :] + rx[1, rows, :].astype(F32)
            product = back * normed
            scaled = back * gains
            first = jnp.mean(scaled, axis=1, keepdims=True)
            second = jnp.mean(scaled * normed, axis=1, keepdims=True)
            upstream = cot[rows, :].astype(F32)
            value = upstream + inverse * (scaled - first - normed * second)
            o_grad[rows, :] = jnp.where(live, value, upstream).astype(BF16)
            return term + jnp.sum(product.reshape(16, 8, D), axis=0)

        term = lax.fori_loop(0, 4, step, jnp.zeros((8, D), F32))
        row = jnp.broadcast_to(jnp.sum(term, axis=0, keepdims=True) * SCALE, (8, D))
        tile = jnp.zeros((8, 128), F32)
        line = lax.broadcasted_iota(jnp.int32, (8, 128), 0)
        lane = lax.broadcasted_iota(jnp.int32, (8, 128), 1)
        for qs in range(8):
            turned = (pltpu.roll(row, D - 96 * qs, 1) if qs else row)[:, 0:128]
            tile = jnp.where(jnp.logical_and(line == qs, lane < 96), turned, tile)
        gz[0] = tile
        send(gz.at[0], gz.at[1], a_s.at[0], a_r.at[0], partner)

    def gain_z_lo():
        got(gz.at[1], a_r.at[0])
        gz[2] = gz[0] + gz[1]
        send(gz.at[2], gz.at[3], a_s.at[1], a_r.at[1], near)

    def gain_x():
        got(gz.at[3], a_r.at[1])
        gxx[x] = gz[2] + gz[3]
        for i in range(1, NX):
            send(gxx.at[x], gxx.at[x], a_s.at[1 + i], a_r.at[1 + i], xp[i - 1])

    def gain_y():
        for i in range(1, NX):
            got(gxx.at[rem(x + NX - i, NX)], a_r.at[1 + i])
        gyy[y] = gxx[0] + gxx[1] + gxx[2] + gxx[3]
        for i in range(1, NY):
            send(gyy.at[y], gyy.at[y], a_s.at[4 + i], a_r.at[4 + i], yp[i - 1])

    def gain_z_hi():
        for i in range(1, NY):
            got(gyy.at[rem(y + NY - i, NY)], a_r.at[4 + i])
        gzz[zh] = gyy[0] + gyy[1] + gyy[2] + gyy[3]
        for i in range(1, NZH):
            send(gzz.at[zh], gzz.at[zh], a_s.at[7 + i], a_r.at[7 + i], zp[i - 1])

    def gain_last():
        for i in range(1, NZH):
            got(gzz.at[rem(zh + NZH - i, NZH)], a_r.at[7 + i])
        o_gain[...] = gzz[0] + gzz[1] + gzz[2] + gzz[3]

    def slot(t, carry):
        @pl.when(t + 1 < C)
        def _():
            forward(t + 1)

        @pl.when(t < C)
        def _():
            grads(t)

        @pl.when(t == C)
        def _():
            tail_out()

        @pl.when(t == C + 1)
        def _():
            tail_rows()

        for late, work in ((1, along_z_lo), (2, along_x), (3, along_y), (4, along_z_hi), (5, back_y)):

            @pl.when(jnp.logical_and(t >= late, t < C + late))
            def _():
                work(t - late)

        return carry

    lax.fori_loop(0, C + 2, slot, 0)
    gain_z_lo()
    along_y(C - 1)
    along_z_hi(C - 2)
    back_y(C - 3)
    gain_x()
    along_z_hi(C - 1)
    gain_y()
    back_y(C - 2)
    gain_z_hi()
    back_y(C - 1)
    gain_last()

    def last(c, carry):
        got(gx.at[c], q6_r.at[c])
        o_g1[1 - k, c] = gx[c]
        for i in range(4):
            got(wg.at[c, q], ag_s.at[c, i])
        for i in range(1, NX):
            got(wg.at[c, q], ag_s.at[c, 3 + i])
        got(r1.at[c, 0:2], q1_s.at[c, 0])
        got(r1.at[c, 2:4], q1_s.at[c, 1])
        for i in range(3):
            got(r2.at[c, i], q2_s.at[c, i])
            got(r3.at[c, i], q3_s.at[c, i])
            got(r4.at[c, zh], q4_s.at[c, i])
            got(fin.at[c, y], q5_s.at[c, i])
        got(gx.at[c], q6_s.at[c])
        return carry

    lax.fori_loop(0, C, last, 0)
    got(wg.at[:, q, mine, :], w_s)
    for i in range(2):
        got(tk.at[here], t_s.at[i])
        got(px.at[i], p_s.at[i])
    for i in range(4):
        got(gsum.at[0], gg_s.at[i])
    got(gt.at[zl], gg_s.at[4])
    for i in range(11):
        got(gz.at[0], a_s.at[i])


def body(tokens, cotangent, live_index, live_count, norm_gain, w_first, w_second):
    images, patches, width = tokens.shape
    tok, cot = tokens.reshape(ROWS, D), cotangent.reshape(ROWS, D)
    gain = jnp.broadcast_to(jnp.pad(norm_gain.astype(F32), (0, 80))[None], (8, 128))
    w1 = w_first.reshape(48, 8, 2, C, HS).transpose(2, 3, 0, 1, 4).reshape(2, C, 48, CW)
    vmem = pl.BlockSpec(memory_space=pltpu.VMEM)
    smem = pl.BlockSpec(memory_space=pltpu.SMEM)
    dma = pltpu.SemaphoreType.DMA
    scratch = [
        pltpu.VMEM((C, 8, SR, CW), BF16),
        pltpu.VMEM((2 * ROWS, D), BF16),
        pltpu.VMEM((2 * ROWS, D), BF16),
        pltpu.VMEM((2 * ROWS, D), BF16),
        pltpu.VMEM((D, 2 * ROWS), BF16),
        pltpu.VMEM((2 * ROWS, D), F32),
        pltpu.VMEM((2 * ROWS, 128), F32),
        pltpu.VMEM((ROWS, 128), F32),
        pltpu.VMEM((C, 2 * ROWS, CW), BF16),
        pltpu.VMEM((C, 2 * ROWS, CW), BF16),
        pltpu.VMEM((C, 2, NX, SR, CW), BF16),
        pltpu.VMEM((C, NX, SR, CW), BF16),
        pltpu.VMEM((C, NX, SR, CW), BF16),
        pltpu.VMEM((C, NX - 1, SR, CW), BF16),
        pltpu.VMEM((C, SR, CW), BF16),
        pltpu.VMEM((C, NY - 1, PR, CW), BF16),
        pltpu.VMEM((C, NZH, PR, CW), BF16),
        pltpu.VMEM((C, NY, PR, CW), BF16),
        pltpu.VMEM((C, PR, CW), BF16),
        pltpu.VMEM((ROWS, D), F32),
        pltpu.VMEM((ROWS, D), F32),
        pltpu.VMEM((2, ROWS, D), BF16),
        pltpu.VMEM((2, ROWS, D), BF16),
        pltpu.VMEM((2, NX, 8, 128), F32),
        pltpu.VMEM((4, 8, 128), F32),
        pltpu.VMEM((4, 8, 128), F32),
        pltpu.VMEM((4, 8, 128), F32),
        pltpu.VMEM((4, 8, 128), F32),
        pltpu.VMEM((4, 8, 128), F32),
        dma((C, 7)), dma((C, 7)),
        dma((C, 2)), dma((C, 2)),
        dma((C, 3)), dma((C, 3)),
        dma((C, 3)), dma((C, 3)),
        dma((C, 3)), dma((C, 3)),
        dma((C, 3)), dma((C, 3)),
        dma((C,)), dma((C,)),
        dma, dma, dma,
        dma((2,)), dma((2,)),
        dma((5,)), dma((5,)),
        dma((2,)), dma((2,)),
        dma((11,)), dma((11,)),
    ]
    out, grad, g1, g2, gg = pl.pallas_call(
        kernel,
        out_shape=(
            jax.ShapeDtypeStruct((ROWS, D), BF16),
            jax.ShapeDtypeStruct((ROWS, D), BF16),
            jax.ShapeDtypeStruct((2, C, 48, CW), BF16),
            jax.ShapeDtypeStruct((192, D), BF16),
            jax.ShapeDtypeStruct((8, 128), F32),
        ),
        in_specs=[vmem, vmem, vmem, smem, vmem, vmem, vmem],
        out_specs=(vmem,) * 5,
        scratch_shapes=scratch,
        compiler_params=pltpu.CompilerParams(
            collective_id=0, has_side_effects=True, vmem_limit_bytes=60 << 20
        ),
        cost_estimate=pl.CostEstimate(flops=14 * 10**9, bytes_accessed=10**7, transcendentals=0),
    )(tok, cot, live_index, live_count, gain, w1, w_second)
    f = lax.axis_index("fsdp")
    grad_first = g1.reshape(2, C, 48, 8, HS).transpose(2, 3, 0, 1, 4).reshape(48, H).astype(F32)
    grad_gain = lax.dynamic_slice(gg, (f // 2, 48 * (f % 2)), (1, 48)).reshape(48)
    return (
        out.reshape(images, patches, width),
        grad.reshape(images, patches, width),
        grad_first,
        g2.astype(F32),
        grad_gain,
    )


def solution(mesh):
    return jax.shard_map(
        body,
        mesh=mesh,
        in_specs=(
            P(("dp", "fsdp"), None, None),
            P(("dp", "fsdp"), None, None),
            P(("dp", "fsdp"), None),
            P(("dp", "fsdp")),
            P("fsdp"),
            P("fsdp", None),
            P("fsdp", None),
        ),
        out_specs=(
            P(("dp", "fsdp"), None, None),
            P(("dp", "fsdp"), None, None),
            P("fsdp", None),
            P("fsdp", None),
            P("fsdp"),
        ),
        check_vma=False,
    )
```

```python
import functools

import jax
import jax.numpy as jnp
from jax import lax
from jax.experimental import pallas as pl
from jax.experimental.pallas import tpu as pltpu
from jax.sharding import PartitionSpec as P

epsilon = 1e-06
root_two_pi = 0.7978845608028654
cubic = 0.044715

MESH = pl.DeviceIdType.MESH
NX, NY, NZH = 4, 4, 4
D, H, ROWS, PATCHES = 768, 3072, 512, 256
AHEAD = 2
C = 6
HS = 192 // C
CW = 8 * HS
R1, R2 = D // 8, D * HS // CW
NB = D // CW
SR = R1 + R2
PR = SR // NY
SCALE = 1.0 / PATCHES
F32, BF16 = jnp.float32, jnp.bfloat16


def rem(a, n):
    return lax.rem(a, jnp.int32(n))


def kernel(tok, cot, idx, cnt, gain, w_in, w2, o_out, o_grad, o_g1, o_g2, o_gain,
           w1, wg, tk, ct, nrm, nt, nf, inv_s, flag_s, hid, bb, buf, r1, s1, r2, s2, r3, r4, fin, gx,
           go, po, pb, px, rx, gt, gsum, gacc, gz, gxx, gyy, gzz,
           ag_s, ag_r, q1_s, q1_r, q2_s, q2_r, q3_s, q3_r, q4_s, q4_r, q5_s, q5_r, q6_s, q6_r,
           w_s, w_r, l_s, t_s, t_r, gg_s, gg_r, p_s, p_r, a_s, a_r):
    dp, f = lax.axis_index("dp"), lax.axis_index("fsdp")
    x, zl, k = lax.div(f, jnp.int32(4)), rem(lax.div(f, jnp.int32(2)), 2), rem(f, 2)
    zh, y = lax.div(dp, jnp.int32(4)), rem(dp, 4)
    z, q = zh * 2 + zl, lax.div(f, jnp.int32(2))

    def dev(x_, y_, z_, k_):
        return (lax.div(z_, jnp.int32(2)) * 4 + y_, x_ * 4 + rem(z_, 2) * 2 + k_)

    z_near = zh * 2 + (1 - zl)
    z_far = rem(z + 8 + 2 * zl - 1, 8)
    partner = dev(x, y, z, 1 - k)
    near, far = dev(x, y, z_near, k), dev(x, y, z_far, k)
    xp = [dev(rem(x + i, NX), y, z, k) for i in range(1, NX)]
    yp = [dev(x, rem(y + i, NY), z, k) for i in range(1, NY)]
    zp = [dev(x, y, rem(z + 2 * i, 8), k) for i in range(1, NZH)]

    def send(src, dst, s_sem, r_sem, to):
        copy = pltpu.make_async_remote_copy(
            src_ref=src, dst_ref=dst, send_sem=s_sem, recv_sem=r_sem, device_id=to, device_id_type=MESH
        )
        copy.start()

    def got(ref, sem):
        pltpu.make_async_copy(ref, ref, sem).wait()

    everyone = [partner, near, far] + xp + yp + zp
    barrier = pltpu.get_barrier_semaphore()
    for peer in everyone:
        pl.semaphore_signal(barrier, inc=1, device_id=peer, device_id_type=MESH)

    lane = lax.broadcasted_iota(jnp.int32, (R1 // 2, 128), 1)
    per = 128 // HS

    def gather_lanes(pieces):
        block = None
        for i, (value, at) in enumerate(pieces):
            turned = value if at == i else pltpu.roll(value, (i - at) * HS % 128, 1)
            block = turned if block is None else jnp.where(lane >= HS * i, turned, block)
        return block

    def hidden_block(core, c, qs):
        return (2 * qs + core) * C + c

    for core in range(2):
        for c in range(C):
            for part in range(CW // 128):
                pieces = []
                for i in range(per):
                    block = hidden_block(core, c, per * part + i)
                    start = block // per * 128
                    pieces.append((w_in[:, start : start + 128].astype(F32), block % per))
                w1[core, c, :, 128 * part : 128 * (part + 1)] = gather_lanes(pieces).astype(BF16)
    gsum[0] = jnp.zeros((8, 128), F32)
    gsum[0, :, 0:48] = jnp.broadcast_to(gain[...].astype(F32), (8, 48))
    gacc[...] = jnp.zeros((8, D), F32)
    pl.semaphore_wait(barrier, len(everyone))

    mine = pl.ds(pl.multiple_of(R1 // 2 * k, 16), R1 // 2)
    other = pl.ds(pl.multiple_of(R1 // 2 * (1 - k), 16), R1 // 2)
    send(w1.at[1 - k], wg.at[:, q, mine, :], w_s, w_r, partner)
    own = pltpu.make_async_copy(w1.at[k], wg.at[:, q, mine, :], l_s)
    own.start()
    g_own = gsum[0]
    g_own = jnp.where(k == 1, pltpu.roll(g_own, 48, 1), g_own)
    gsum[0] = g_own
    send(gsum.at[0], gsum.at[1], gg_s.at[0], gg_r.at[0], partner)
    for c in range(C):
        for n in range(NB):
            wg[c, q, R1 + HS * n : R1 + HS * (n + 1), :] = w2[HS * c : HS * (c + 1), CW * n : CW * (n + 1)]
    own.wait()
    got(wg.at[:, q, other, :], w_r)

    def first_sends(c, carry):
        for i in range(1, NX):
            send(wg.at[c, q], wg.at[c, q], ag_s.at[c, i - 1], ag_r.at[c, i - 1], xp[i - 1])
        to = tuple(jnp.where(x < 2, a, b) for a, b in zip(near, far))
        send(wg.at[c, q], wg.at[c, q], ag_s.at[c, 3], ag_r.at[c, 3 + x], to)
        return carry

    lax.fori_loop(0, AHEAD, first_sends, 0)

    got(gsum.at[1], gg_r.at[0])
    gt[zl, x] = gsum[0] + gsum[1]
    for i in range(1, NX):
        send(gt.at[zl, x], gt.at[zl, x], gg_s.at[i], gg_r.at[i], xp[i - 1])

    for image in range(2):
        at = lax.broadcasted_iota(jnp.int32, (PATCHES, PATCHES), 0)
        place = lax.broadcasted_iota(jnp.int32, (PATCHES, PATCHES), 1)
        hit = jnp.where(
            jnp.logical_and(idx[image : image + 1, :] == at, place < cnt[image]), 1.0, 0.0
        ).astype(F32)
        flag = jnp.max(hit, axis=1, keepdims=True)
        rows = slice(PATCHES * image, PATCHES * (image + 1))
        flag_s[rows, :] = jnp.broadcast_to(flag, (PATCHES, 128))
        to = pl.ds(pl.multiple_of(ROWS * k + PATCHES * image, PATCHES), PATCHES)
        tk[to, :] = jnp.where(flag > 0, tok[rows, :].astype(F32), 0.0).astype(BF16)
        ct[to, :] = jnp.where(flag > 0, cot[rows, :].astype(F32), 0.0).astype(BF16)
    here = pl.ds(pl.multiple_of(ROWS * k, ROWS), ROWS)
    there = pl.ds(pl.multiple_of(ROWS * (1 - k), ROWS), ROWS)
    send(tk.at[here], tk.at[here], t_s.at[0], t_r.at[0], partner)
    send(ct.at[here], ct.at[here], t_s.at[1], t_r.at[1], partner)

    def forward(c):
        for i in range(1, NX):
            xs = rem(x + NX - i, NX)
            qs = xs * 2 + zl
            got(wg.at[c, qs], ag_r.at[c, i - 1])
            to = tuple(jnp.where(xs < 2, a, b) for a, b in zip(near, far))
            send(wg.at[c, qs], wg.at[c, qs], ag_s.at[c, 3 + i], ag_r.at[c, 3 + xs], to)

    for i in range(1, NX):
        got(gt.at[zl, rem(x + NX - i, NX)], gg_r.at[i])
    send(gt.at[zl], gt.at[zl], gg_s.at[4], gg_r.at[4], near)
    forward(0)
    got(gt.at[1 - zl], gg_r.at[4])
    got(tk.at[there], t_r.at[0])
    got(ct.at[there], t_r.at[1])

    def gain_row():
        total = jnp.zeros((8, D), F32)
        for qs in range(8):
            tile = jnp.concatenate([gt[qs % 2, qs // 2], jnp.zeros((8, D - 128), F32)], axis=1)
            total = total + (pltpu.roll(tile, 96 * qs, 1) if qs else tile)
        return total[0:1, :]

    gains = gain_row()

    def norm_step(m, carry):
        rows = pl.ds(pl.multiple_of(256 * m, 256), 256)
        values = tk[rows, :].astype(F32)
        center = jnp.mean(values, axis=1, keepdims=True)
        values = values - center
        spread = jnp.mean(values * values, axis=1, keepdims=True)
        inverse = lax.rsqrt(spread + epsilon)
        normed = values * inverse
        nf[rows, :] = normed
        inv_s[rows, :] = jnp.broadcast_to(inverse, (256, 128))
        normal = normed * gains
        nrm[rows, :] = normal.astype(BF16)
        nt[:, rows] = jnp.transpose(normal).astype(BF16)
        return carry

    lax.fori_loop(0, 4, norm_step, 0)

    def first_of(c):
        return wg[c, :, 0:R1, :].reshape(D, CW)

    def second_of(c, n):
        return wg[c, :, R1 + HS * n : R1 + HS * (n + 1), :].reshape(CW, CW)

    def grads(c):
        for i in range(4):
            qs = 2 * i + 1 - zl
            got(wg.at[c, qs], ag_r.at[c, 3 + i])

        def step(m, carry):
            rows = pl.ds(pl.multiple_of(256 * m, 256), 256)
            before = jnp.dot(nrm[rows, :], first_of(c), preferred_element_type=F32)
            back = jnp.zeros((256, CW), F32)
            for n in range(NB):
                back = back + lax.dot_general(
                    ct[rows, CW * n : CW * (n + 1)], second_of(c, n), (((1,), (1,)), ((), ())),
                    preferred_element_type=F32,
                )
            square = before * before
            tangent = jnp.tanh(before * (root_two_pi + (root_two_pi * cubic) * square))
            half = 0.5 + 0.5 * tangent
            hid[c, rows, :] = (before * half).astype(BF16)
            slope = half + (0.5 * before) * (1.0 - tangent * tangent) * (
                root_two_pi + (3.0 * cubic * root_two_pi) * square
            )
            bb[c, rows, :] = (back * slope).astype(BF16)
            return carry

        lax.fori_loop(0, 4, step, 0)
        for part in range(2):
            term = jnp.dot(nt[384 * part : 384 * (part + 1), :], bb[c], preferred_element_type=F32)
            own_rows = wg[c, 4 * part : 4 * (part + 1), 0:R1, :].reshape(384, CW)
            product = term * own_rows.astype(F32)
            high = product.astype(BF16)
            low = (product - high.astype(F32)).astype(BF16)
            ones = jnp.ones((8, CW), BF16)
            line_sum = jnp.zeros((8, 384), F32)
            for share in (high, low):
                line_sum = line_sum + lax.dot_general(
                    ones, share, (((1,), (1,)), ((), ())), preferred_element_type=F32
                )
            gacc[:, 384 * part : 384 * (part + 1)] += line_sum
            term = (term * SCALE).astype(BF16)
            for i in range(4):
                qs = 4 * part + i
                buf[c, qs % 2, qs // 2, 0:R1, :] = term[R1 * i : R1 * (i + 1), :]
        for n in range(NB):
            term = lax.dot_general(
                hid[c], ct[:, CW * n : CW * (n + 1)], (((0,), (0,)), ((), ())), preferred_element_type=F32
            )
            term = (term * SCALE).astype(BF16)
            for qs in range(8):
                buf[c, qs % 2, qs // 2, R1 + HS * n : R1 + HS * (n + 1), :] = term[HS * qs : HS * (qs + 1), :]
        send(buf.at[c, 1 - zl, 0:2], r1.at[c, 0:2], q1_s.at[c, 0], q1_r.at[c, 0], near)
        send(buf.at[c, 1 - zl, 2:4], r1.at[c, 2:4], q1_s.at[c, 1], q1_r.at[c, 1], far)

    def along_z_lo(c):
        got(r1.at[c, 0:2], q1_r.at[c, 0])
        got(r1.at[c, 2:4], q1_r.at[c, 1])
        for i in range(NX):
            s1[c, i] = (buf[c, zl, i].astype(F32) + r1[c, i].astype(F32)).astype(BF16)
        for i in range(1, NX):
            send(s1.at[c, rem(x + i, NX)], r2.at[c, i - 1], q2_s.at[c, i - 1], q2_r.at[c, i - 1], xp[i - 1])

    def along_x(c):
        for i in range(NX - 1):
            got(r2.at[c, i], q2_r.at[c, i])
        total = s1[c, x].astype(F32)
        for i in range(NX - 1):
            total = total + r2[c, i].astype(F32)
        s2[c] = total.astype(BF16)
        for i in range(1, NY):
            part = pl.ds(pl.multiple_of(PR * rem(y + i, NY), 16), PR)
            send(s2.at[c, part], r3.at[c, i - 1], q3_s.at[c, i - 1], q3_r.at[c, i - 1], yp[i - 1])

    def along_y(c):
        for i in range(NY - 1):
            got(r3.at[c, i], q3_r.at[c, i])
        total = s2[c, pl.ds(pl.multiple_of(PR * y, 16), PR), :].astype(F32)
        for i in range(NY - 1):
            total = total + r3[c, i].astype(F32)
        r4[c, zh] = total.astype(BF16)
        for i in range(1, NZH):
            send(r4.at[c, zh], r4.at[c, zh], q4_s.at[c, i - 1], q4_r.at[c, i - 1], zp[i - 1])

    def along_z_hi(c):
        for i in range(1, NZH):
            got(r4.at[c, rem(zh + NZH - i, NZH)], q4_r.at[c, i - 1])
        total = r4[c, 0].astype(F32)
        for i in range(1, NZH):
            total = total + r4[c, i].astype(F32)
        fin[c, y] = total.astype(BF16)
        for i in range(1, NY):
            send(fin.at[c, y], fin.at[c, y], q5_s.at[c, i - 1], q5_r.at[c, i - 1], yp[i - 1])

    def back_y(c):
        for i in range(1, NY):
            got(fin.at[c, rem(y + NY - i, NY)], q5_r.at[c, i - 1])
        send(fin.at[c, 1 - k], gx.at[c], q6_s.at[c], q6_r.at[c], partner)
        go[k, c] = fin[c, k].astype(F32)
        second = fin[c, 2:4].reshape(R2, CW)
        rows = pl.ds(pl.multiple_of(HS * c, HS), HS)
        for n in range(NB):
            o_g2[rows, CW * n : CW * (n + 1)] = second[HS * n : HS * (n + 1), :].astype(F32)

    def out_rows(start):
        rows = pl.ds(pl.multiple_of(start, 256), 256)
        parts = []
        for n in range(NB):
            total = jnp.zeros((256, CW), F32)
            for c in range(C):
                total = total + jnp.dot(hid[c, rows, :], second_of(c, n), preferred_element_type=F32)
            parts.append(total)
        return parts

    def back_rows(start):
        rows = pl.ds(pl.multiple_of(start, 256), 256)
        total = jnp.zeros((256, D), F32)
        for c in range(C):
            total = total + lax.dot_general(
                bb[c, rows, :], first_of(c), (((1,), (1,)), ((), ())), preferred_element_type=F32
            )
        return total

    def tail_out():
        def step(m, carry):
            rows = pl.ds(pl.multiple_of(256 * m, 256), 256)
            for n, part in enumerate(out_rows(ROWS * (1 - k) + 256 * m)):
                px[0, rows, CW * n : CW * (n + 1)] = part.astype(BF16)
            px[1, rows, :] = back_rows(ROWS * (1 - k) + 256 * m).astype(BF16)
            return carry

        lax.fori_loop(0, 2, step, 0)
        for i in range(2):
            send(px.at[i], rx.at[i], p_s.at[i], p_r.at[i], partner)

        def step(m, carry):
            rows = pl.ds(pl.multiple_of(256 * m, 256), 256)
            for n, part in enumerate(out_rows(ROWS * k + 256 * m)):
                po[rows, CW * n : CW * (n + 1)] = part
            pb[rows, :] = back_rows(ROWS * k + 256 * m)
            return carry

        lax.fori_loop(0, 2, step, 0)

    def tail_rows():
        for i in range(2):
            got(rx.at[i], p_r.at[i])

        def step(m, carry):
            rows = pl.ds(pl.multiple_of(128 * m, 128), 128)
            at = pl.ds(pl.multiple_of(ROWS * k + 128 * m, 128), 128)
            live = flag_s[rows, :][:, 0:1] > 0
            plain = tok[rows, :].astype(F32)
            mixed = plain + (po[rows, :] + rx[0, rows, :].astype(F32))
            o_out[rows, :] = jnp.where(live, mixed, plain).astype(BF16)
            normed = nf[at, :]
            inverse = inv_s[at, :][:, 0:1]
            back = pb[rows, :] + rx[1, rows, :].astype(F32)
            scaled = back * gains
            first = jnp.mean(scaled, axis=1, keepdims=True)
            second = jnp.mean(scaled * normed, axis=1, keepdims=True)
            upstream = cot[rows, :].astype(F32)
            value = upstream + inverse * (scaled - first - normed * second)
            o_grad[rows, :] = jnp.where(live, value, upstream).astype(BF16)
            return carry

        lax.fori_loop(0, 4, step, 0)

    def gain_core():
        row = gacc[...] * SCALE / gains
        tile = jnp.zeros((8, 128), F32)
        line = lax.broadcasted_iota(jnp.int32, (8, 128), 0)
        for qs in range(8):
            turned = (pltpu.roll(row, D - 96 * qs, 1) if qs else row)[:, 0:128]
            tile = jnp.where(line == qs, turned, tile)
        gz[0] = tile
        send(gz.at[0], gz.at[1], a_s.at[0], a_r.at[0], partner)

    def gain_z_lo():
        got(gz.at[1], a_r.at[0])
        gz[2] = gz[0] + gz[1]
        send(gz.at[2], gz.at[3], a_s.at[1], a_r.at[1], near)

    def gain_x():
        got(gz.at[3], a_r.at[1])
        gxx[x] = gz[2] + gz[3]
        for i in range(1, NX):
            send(gxx.at[x], gxx.at[x], a_s.at[1 + i], a_r.at[1 + i], xp[i - 1])

    def gain_y():
        for i in range(1, NX):
            got(gxx.at[rem(x + NX - i, NX)], a_r.at[1 + i])
        gyy[y] = gxx[0] + gxx[1] + gxx[2] + gxx[3]
        for i in range(1, NY):
            send(gyy.at[y], gyy.at[y], a_s.at[4 + i], a_r.at[4 + i], yp[i - 1])

    def gain_z_hi():
        for i in range(1, NY):
            got(gyy.at[rem(y + NY - i, NY)], a_r.at[4 + i])
        gzz[zh] = gyy[0] + gyy[1] + gyy[2] + gyy[3]
        for i in range(1, NZH):
            send(gzz.at[zh], gzz.at[zh], a_s.at[7 + i], a_r.at[7 + i], zp[i - 1])

    def gain_last():
        for i in range(1, NZH):
            got(gzz.at[rem(zh + NZH - i, NZH)], a_r.at[7 + i])
        total = gzz[0] + gzz[1] + gzz[2] + gzz[3]
        line = lax.broadcasted_iota(jnp.int32, (8, 128), 0)
        row = jnp.sum(jnp.where(line == q, total, 0.0), axis=0, keepdims=True)
        row = jnp.broadcast_to(row, (8, 128))
        row = jnp.where(k == 1, pltpu.roll(row, 80, 1), row)
        o_gain[...] = row[0:1, 0:48]

    def slot(t, carry):
        @pl.when(t + AHEAD < C)
        def _():
            first_sends(t + AHEAD, 0)

        @pl.when(t + 1 < C)
        def _():
            forward(t + 1)

        @pl.when(t < C)
        def _():
            grads(t)

        @pl.when(t == C)
        def _():
            gain_core()
            tail_out()

        @pl.when(t == C + 1)
        def _():
            tail_rows()

        for late, work in ((1, along_z_lo), (2, along_x), (3, along_y), (4, along_z_hi), (5, back_y)):

            @pl.when(jnp.logical_and(t >= late, t < C + late))
            def _():
                work(t - late)

        return carry

    lax.fori_loop(0, C + 2, slot, 0)
    gain_z_lo()
    along_y(C - 1)
    along_z_hi(C - 2)
    back_y(C - 3)
    gain_x()
    along_z_hi(C - 1)
    gain_y()
    back_y(C - 2)
    gain_z_hi()
    back_y(C - 1)
    gain_last()

    def last(c, carry):
        got(gx.at[c], q6_r.at[c])
        go[1 - k, c] = gx[c].astype(F32)
        for i in range(4):
            got(wg.at[c, q], ag_s.at[c, i])
        for i in range(1, NX):
            got(wg.at[c, q], ag_s.at[c, 3 + i])
        got(r1.at[c, 0:2], q1_s.at[c, 0])
        got(r1.at[c, 2:4], q1_s.at[c, 1])
        for i in range(3):
            got(r2.at[c, i], q2_s.at[c, i])
            got(r3.at[c, i], q3_s.at[c, i])
            got(r4.at[c, zh], q4_s.at[c, i])
            got(fin.at[c, y], q5_s.at[c, i])
        got(gx.at[c], q6_s.at[c])
        return carry

    lax.fori_loop(0, C, last, 0)
    place = {}
    for core in range(2):
        for c in range(C):
            for qs in range(8):
                place[hidden_block(core, c, qs)] = (core, c, qs)
    for block in range(H // 128):
        pieces = []
        for i in range(per):
            core, c, qs = place[per * block + i]
            start = qs // per * 128
            pieces.append((go[core, c, :, start : start + 128], qs % per))
        o_g1[:, 128 * block : 128 * (block + 1)] = gather_lanes(pieces)
    got(wg.at[:, q, mine, :], w_s)
    for i in range(2):
        got(tk.at[here], t_s.at[i])
        got(px.at[i], p_s.at[i])
    for i in range(4):
        got(gsum.at[0], gg_s.at[i])
    got(gt.at[zl], gg_s.at[4])
    for i in range(11):
        got(gz.at[0], a_s.at[i])


def body(tokens, cotangent, live_index, live_count, norm_gain, w_first, w_second):
    images, patches, width = tokens.shape
    tok, cot = tokens.reshape(ROWS, D), cotangent.reshape(ROWS, D)
    vmem = pl.BlockSpec(memory_space=pltpu.VMEM)
    smem = pl.BlockSpec(memory_space=pltpu.SMEM)
    dma = pltpu.SemaphoreType.DMA
    scratch = [
        pltpu.VMEM((2, C, R1 // 2, CW), BF16),
        pltpu.VMEM((C, 8, SR, CW), BF16),
        pltpu.VMEM((2 * ROWS, D), BF16),
        pltpu.VMEM((2 * ROWS, D), BF16),
        pltpu.VMEM((2 * ROWS, D), BF16),
        pltpu.VMEM((D, 2 * ROWS), BF16),
        pltpu.VMEM((2 * ROWS, D), F32),
        pltpu.VMEM((2 * ROWS, 128), F32),
        pltpu.VMEM((ROWS, 128), F32),
        pltpu.VMEM((C, 2 * ROWS, CW), BF16),
        pltpu.VMEM((C, 2 * ROWS, CW), BF16),
        pltpu.VMEM((C, 2, NX, SR, CW), BF16),
        pltpu.VMEM((C, NX, SR, CW), BF16),
        pltpu.VMEM((C, NX, SR, CW), BF16),
        pltpu.VMEM((C, NX - 1, SR, CW), BF16),
        pltpu.VMEM((C, SR, CW), BF16),
        pltpu.VMEM((C, NY - 1, PR, CW), BF16),
        pltpu.VMEM((C, NZH, PR, CW), BF16),
        pltpu.VMEM((C, NY, PR, CW), BF16),
        pltpu.VMEM((C, PR, CW), BF16),
        pltpu.VMEM((2, C, R1 // 2, CW), F32),
        pltpu.VMEM((ROWS, D), F32),
        pltpu.VMEM((ROWS, D), F32),
        pltpu.VMEM((2, ROWS, D), BF16),
        pltpu.VMEM((2, ROWS, D), BF16),
        pltpu.VMEM((2, NX, 8, 128), F32),
        pltpu.VMEM((4, 8, 128), F32),
        pltpu.VMEM((8, D), F32),
        pltpu.VMEM((4, 8, 128), F32),
        pltpu.VMEM((4, 8, 128), F32),
        pltpu.VMEM((4, 8, 128), F32),
        pltpu.VMEM((4, 8, 128), F32),
        dma((C, 7)), dma((C, 7)),
        dma((C, 2)), dma((C, 2)),
        dma((C, 3)), dma((C, 3)),
        dma((C, 3)), dma((C, 3)),
        dma((C, 3)), dma((C, 3)),
        dma((C, 3)), dma((C, 3)),
        dma((C,)), dma((C,)),
        dma, dma, dma,
        dma((2,)), dma((2,)),
        dma((5,)), dma((5,)),
        dma((2,)), dma((2,)),
        dma((11,)), dma((11,)),
    ]
    out, grad, g1, g2, gg = pl.pallas_call(
        kernel,
        out_shape=(
            jax.ShapeDtypeStruct((ROWS, D), BF16),
            jax.ShapeDtypeStruct((ROWS, D), BF16),
            jax.ShapeDtypeStruct((48, H), F32),
            jax.ShapeDtypeStruct((192, D), F32),
            jax.ShapeDtypeStruct((1, 48), F32),
        ),
        in_specs=[vmem, vmem, vmem, smem, vmem, vmem, vmem],
        out_specs=(vmem,) * 5,
        scratch_shapes=scratch,
        compiler_params=pltpu.CompilerParams(
            collective_id=0, has_side_effects=True, vmem_limit_bytes=60 << 20
        ),
        cost_estimate=pl.CostEstimate(flops=14 * 10**9, bytes_accessed=10**7, transcendentals=0),
    )(tok, cot, live_index, live_count, norm_gain.reshape(1, 48), w_first, w_second)
    return (
        out.reshape(images, patches, width),
        grad.reshape(images, patches, width),
        g1,
        g2,
        gg.reshape(48),
    )


def solution(mesh):
    return jax.shard_map(
        body,
        mesh=mesh,
        in_specs=(
            P(("dp", "fsdp"), None, None),
            P(("dp", "fsdp"), None, None),
            P(("dp", "fsdp"), None),
            P(("dp", "fsdp")),
            P("fsdp"),
            P("fsdp", None),
            P("fsdp", None),
        ),
        out_specs=(
            P(("dp", "fsdp"), None, None),
            P(("dp", "fsdp"), None, None),
            P("fsdp", None),
            P("fsdp", None),
            P("fsdp"),
        ),
        check_vma=False,
    )
```

```python
import functools

import jax
import jax.numpy as jnp
from jax import lax
from jax.experimental import pallas as pl
from jax.experimental.pallas import tpu as pltpu
from jax.sharding import PartitionSpec as P

epsilon = 1e-06
root_two_pi = 0.7978845608028654
cubic = 0.044715

MESH = pl.DeviceIdType.MESH
NX, NY, NZH = 4, 4, 4
D, H, ROWS, PATCHES = 768, 3072, 512, 256
SPLIT = 4
C = 6
HS = 192 // C
CW = 8 * HS
R1, R2 = D // 8, D * HS // CW
NB = D // CW
SR = R1 + R2
PR = SR // NY
SCALE = 1.0 / PATCHES
F32, BF16 = jnp.float32, jnp.bfloat16


def rem(a, n):
    return lax.rem(a, jnp.int32(n))


def kernel(tok, cot, idx, cnt, gain, w_in, w2, o_out, o_grad, o_g1, o_g2, o_gain,
           w1, wg, tk, ct, nrm, nt, nf, inv_s, flag_s, hid, bb, buf, r1, s1, r2, s2, r3, r4, fin, gx,
           go, po, pb, px, rx, gt, gsum, gacc, gz, gxx, gyy, gzz,
           ag_s, ag_r, az_s, az_r, ay_s, ay_r, q1_s, q1_r, q2_s, q2_r, q3_s, q3_r, q4_s, q4_r, q5_s, q5_r, q6_s, q6_r,
           w_s, w_r, t_s, t_r, gg_s, gg_r, p_s, p_r, a_s, a_r):
    dp, f = lax.axis_index("dp"), lax.axis_index("fsdp")
    x, zl, k = lax.div(f, jnp.int32(4)), rem(lax.div(f, jnp.int32(2)), 2), rem(f, 2)
    zh, y = lax.div(dp, jnp.int32(4)), rem(dp, 4)
    z, q = zh * 2 + zl, lax.div(f, jnp.int32(2))

    def dev(x_, y_, z_, k_):
        return (lax.div(z_, jnp.int32(2)) * 4 + y_, x_ * 4 + rem(z_, 2) * 2 + k_)

    z_near = zh * 2 + (1 - zl)
    z_far = rem(z + 8 + 2 * zl - 1, 8)
    partner = dev(x, y, z, 1 - k)
    near, far = dev(x, y, z_near, k), dev(x, y, z_far, k)
    xp = [dev(rem(x + i, NX), y, z, k) for i in range(1, NX)]
    yp = [dev(x, rem(y + i, NY), z, k) for i in range(1, NY)]
    zp = [dev(x, y, rem(z + 2 * i, 8), k) for i in range(1, NZH)]

    def send(src, dst, s_sem, r_sem, to):
        copy = pltpu.make_async_remote_copy(
            src_ref=src, dst_ref=dst, send_sem=s_sem, recv_sem=r_sem, device_id=to, device_id_type=MESH
        )
        copy.start()

    def got(ref, sem):
        pltpu.make_async_copy(ref, ref, sem).wait()

    everyone = [partner, near, far] + xp + yp + zp
    barrier = pltpu.get_barrier_semaphore()
    for peer in everyone:
        pl.semaphore_signal(barrier, inc=1, device_id=peer, device_id_type=MESH)

    lane = lax.broadcasted_iota(jnp.int32, (R1 // 2, 128), 1)
    per = 128 // HS

    def gather_lanes(pieces):
        block = None
        for i, (value, at) in enumerate(pieces):
            turned = value if at == i else pltpu.roll(value, (i - at) * HS % 128, 1)
            block = turned if block is None else jnp.where(lane >= HS * i, turned, block)
        return block

    def hidden_block(core, c, qs):
        return (2 * qs + core) * C + c

    gains_own = jnp.broadcast_to(gain[...].astype(F32), (8, 48))
    gsum[0] = jnp.zeros((8, 128), F32)
    for core in range(2):

        @pl.when(k == core)
        def _():
            gsum[0, :, 48 * core : 48 * (core + 1)] = gains_own

    gacc[...] = jnp.zeros((8, D), F32)
    y_odd = rem(y, 2) == 1

    @pl.when(jnp.logical_not(y_odd))
    def _():
        for core in range(2):
            for c in range(C):
                for part in range(CW // 128):
                    pieces = []
                    for i in range(per):
                        block = hidden_block(core, c, per * part + i)
                        start = block // per * 128
                        pieces.append((w_in[:, start : start + 128].astype(F32), block % per))
                    w1[core, c, :, 128 * part : 128 * (part + 1)] = gather_lanes(pieces).astype(BF16)

    @pl.when(y_odd)
    def _():
        for c in range(C):
            for n in range(NB):
                wg[c, zl, x, R1 + HS * n : R1 + HS * (n + 1), :] = w2[
                    HS * c : HS * (c + 1), CW * n : CW * (n + 1)
                ]

    pl.semaphore_wait(barrier, len(everyone))

    send(gsum.at[0], gsum.at[1], gg_s.at[0], gg_r.at[0], partner)
    mine = pl.ds(pl.multiple_of(R1 // 2 * k, 16), R1 // 2)
    other = pl.ds(pl.multiple_of(R1 // 2 * (1 - k), 16), R1 // 2)

    @pl.when(jnp.logical_not(y_odd))
    def _():
        send(w1.at[1 - k], wg.at[:, zl, x, mine, :], w_s, w_r, partner)
        for c in range(C):
            wg[c, zl, x, mine, :] = w1[k, c]
        got(wg.at[:, zl, x, other, :], w_r)

    half = rem(y, 2)
    my_half = pl.ds(pl.multiple_of(SR // 2 * half, 16), SR // 2)
    its_half = pl.ds(pl.multiple_of(SR // 2 * (1 - half), 16), SR // 2)

    def pick(cond, a, b):
        return tuple(jnp.where(cond, i, j) for i, j in zip(a, b))

    def first_sends(c):
        block = wg.at[c, zl, x, my_half]
        for i in range(1, NX):
            send(block, block, ag_s.at[c, i - 1], ag_r.at[c, i - 1], xp[i - 1])

    first_sends(0)

    got(gsum.at[1], gg_r.at[0])
    gt[zl, x] = gsum[0] + gsum[1]
    for i in range(1, NX):
        send(gt.at[zl, x], gt.at[zl, x], gg_s.at[i], gg_r.at[i], xp[i - 1])

    for image in range(2):
        at = lax.broadcasted_iota(jnp.int32, (PATCHES, PATCHES), 0)
        place = lax.broadcasted_iota(jnp.int32, (PATCHES, PATCHES), 1)
        hit = jnp.where(
            jnp.logical_and(idx[image : image + 1, :] == at, place < cnt[image]), 1.0, 0.0
        ).astype(F32)
        flag = jnp.max(hit, axis=1, keepdims=True)
        rows = slice(PATCHES * image, PATCHES * (image + 1))
        flag_s[rows, :] = jnp.broadcast_to(flag, (PATCHES, 128))
        to = pl.ds(pl.multiple_of(ROWS * k + PATCHES * image, PATCHES), PATCHES)
        tk[to, :] = jnp.where(flag > 0, tok[rows, :].astype(F32), 0.0).astype(BF16)
        ct[to, :] = jnp.where(flag > 0, cot[rows, :].astype(F32), 0.0).astype(BF16)
    here = pl.ds(pl.multiple_of(ROWS * k, ROWS), ROWS)
    there = pl.ds(pl.multiple_of(ROWS * (1 - k), ROWS), ROWS)
    send(tk.at[here], tk.at[here], t_s.at[0], t_r.at[0], partner)
    send(ct.at[here], ct.at[here], t_s.at[1], t_r.at[1], partner)

    def swap(c, kind, at):
        for i, to in enumerate((yp[0], yp[2])):
            block = wg.at[c, kind, 2 * i : 2 * i + 2, my_half]
            send(block, block, ay_s.at[c, 2 * at + i], ay_r.at[c, 2 * at + i], to)

    def forward_x(c):
        for i in range(1, NX):
            got(wg.at[c, zl, rem(x + NX - i, NX), my_half], ag_r.at[c, i - 1])
        for i, to in enumerate((near, far)):
            block = wg.at[c, zl, 2 * i : 2 * i + 2, my_half]
            send(block, block, az_s.at[c, i], az_r.at[c, i], to)
        swap(c, zl, 0)

    def forward_z(c):
        for i in range(2):
            got(wg.at[c, 1 - zl, 2 * i : 2 * i + 2, my_half], az_r.at[c, i])
        swap(c, 1 - zl, 1)

    for i in range(1, NX):
        got(gt.at[zl, rem(x + NX - i, NX)], gg_r.at[i])
    send(gt.at[zl], gt.at[zl], gg_s.at[4], gg_r.at[4], near)
    forward_x(0)
    first_sends(1)
    got(gt.at[1 - zl], gg_r.at[4])
    got(tk.at[there], t_r.at[0])
    got(ct.at[there], t_r.at[1])

    def gain_row():
        total = jnp.zeros((8, D), F32)
        for qs in range(8):
            tile = jnp.concatenate([gt[qs % 2, qs // 2], jnp.zeros((8, D - 128), F32)], axis=1)
            total = total + (pltpu.roll(tile, 96 * qs, 1) if qs else tile)
        return total[0:1, :]

    gains = gain_row()

    def norm_step(m, carry):
        rows = pl.ds(pl.multiple_of(256 * m, 256), 256)
        values = tk[rows, :].astype(F32)
        center = jnp.mean(values, axis=1, keepdims=True)
        values = values - center
        spread = jnp.mean(values * values, axis=1, keepdims=True)
        inverse = lax.rsqrt(spread + epsilon)
        normed = values * inverse
        nf[rows, :] = normed
        inv_s[rows, :] = jnp.broadcast_to(inverse, (256, 128))
        normal = normed * gains
        nrm[rows, :] = normal.astype(BF16)
        nt[:, rows] = jnp.transpose(normal).astype(BF16)
        return carry

    lax.fori_loop(0, 4, norm_step, 0)
    forward_z(0)
    forward_x(1)
    first_sends(2)

    def first_of(c):
        return jnp.concatenate([wg[c, qs % 2, qs // 2, 0:R1, :] for qs in range(8)], axis=0)

    def second_of(c, n):
        rows = slice(R1 + HS * n, R1 + HS * (n + 1))
        return jnp.concatenate([wg[c, qs % 2, qs // 2, rows, :] for qs in range(8)], axis=0)

    def grads(c):
        for i in range(4):
            kind, at = zl if i < 2 else 1 - zl, i % 2
            got(wg.at[c, kind, 2 * at : 2 * at + 2, its_half], ay_r.at[c, i])

        def step(m, carry):
            rows = pl.ds(pl.multiple_of(256 * m, 256), 256)
            before = jnp.dot(nrm[rows, :], first_of(c), preferred_element_type=F32)
            back = jnp.zeros((256, CW), F32)
            for n in range(NB):
                back = back + lax.dot_general(
                    ct[rows, CW * n : CW * (n + 1)], second_of(c, n), (((1,), (1,)), ((), ())),
                    preferred_element_type=F32,
                )
            square = before * before
            tangent = jnp.tanh(before * (root_two_pi + (root_two_pi * cubic) * square))
            half = 0.5 + 0.5 * tangent
            hid[c, rows, :] = (before * half).astype(BF16)
            slope = half + (0.5 * before) * (1.0 - tangent * tangent) * (
                root_two_pi + (3.0 * cubic * root_two_pi) * square
            )
            bb[c, rows, :] = (back * slope).astype(BF16)
            return carry

        lax.fori_loop(0, 4, step, 0)
        for part in range(2):
            term = jnp.dot(nt[384 * part : 384 * (part + 1), :], bb[c], preferred_element_type=F32)
            own_rows = jnp.concatenate(
                [wg[c, qs % 2, qs // 2, 0:R1, :] for qs in range(4 * part, 4 * part + 4)], axis=0
            )
            product = term * own_rows.astype(F32)
            high = product.astype(BF16)
            low = (product - high.astype(F32)).astype(BF16)
            ones = jnp.ones((8, CW), BF16)
            line_sum = jnp.zeros((8, 384), F32)
            for share in (high, low):
                line_sum = line_sum + lax.dot_general(
                    ones, share, (((1,), (1,)), ((), ())), preferred_element_type=F32
                )
            gacc[:, 384 * part : 384 * (part + 1)] += line_sum
            term = (term * SCALE).astype(BF16)
            for i in range(4):
                qs = 4 * part + i
                buf[c, qs % 2, qs // 2, 0:R1, :] = term[R1 * i : R1 * (i + 1), :]
        for n in range(NB):
            term = lax.dot_general(
                hid[c], ct[:, CW * n : CW * (n + 1)], (((0,), (0,)), ((), ())), preferred_element_type=F32
            )
            term = (term * SCALE).astype(BF16)
            for qs in range(8):
                buf[c, qs % 2, qs // 2, R1 + HS * n : R1 + HS * (n + 1), :] = term[HS * qs : HS * (qs + 1), :]
        send(buf.at[c, 1 - zl, 0:2], r1.at[c, 0:2], q1_s.at[c, 0], q1_r.at[c, 0], near)
        send(buf.at[c, 1 - zl, 2:4], r1.at[c, 2:4], q1_s.at[c, 1], q1_r.at[c, 1], far)

    def along_z_lo(c):
        got(r1.at[c, 0:2], q1_r.at[c, 0])
        got(r1.at[c, 2:4], q1_r.at[c, 1])
        for i in range(NX):
            s1[c, i] = (buf[c, zl, i].astype(F32) + r1[c, i].astype(F32)).astype(BF16)
        for i in range(1, NX):
            send(s1.at[c, rem(x + i, NX)], r2.at[c, i - 1], q2_s.at[c, i - 1], q2_r.at[c, i - 1], xp[i - 1])

    def along_x(c):
        for i in range(NX - 1):
            got(r2.at[c, i], q2_r.at[c, i])
        total = s1[c, x].astype(F32)
        for i in range(NX - 1):
            total = total + r2[c, i].astype(F32)
        s2[c] = total.astype(BF16)
        for i in range(1, NY):
            part = pl.ds(pl.multiple_of(PR * rem(y + i, NY), 16), PR)
            send(s2.at[c, part], r3.at[c, i - 1], q3_s.at[c, i - 1], q3_r.at[c, i - 1], yp[i - 1])

    def along_y(c, last=False):
        for i in range(NY - 1):
            got(r3.at[c, i], q3_r.at[c, i])
        total = s2[c, pl.ds(pl.multiple_of(PR * y, 16), PR), :].astype(F32)
        for i in range(NY - 1):
            total = total + r3[c, i].astype(F32)
        if last:
            r4[c, zh] = total.astype(BF16)
            for i in range(1, NZH):
                send(r4.at[c, zh], r4.at[c, zh], q4_s.at[c, i - 1], q4_r.at[c, i - 1], zp[i - 1])
        else:
            r4[c, 0] = total.astype(BF16)
            to = pick(jnp.logical_xor(rem(zh, 2) == 0, rem(c, 2) == 0), zp[2], zp[0])
            send(r4.at[c, 0], r4.at[c, 1], q4_s.at[c, 0], q4_r.at[c, 0], to)

    def spread_y(c, total):
        fin[c, y] = total.astype(BF16)
        for i in range(1, NY):
            send(fin.at[c, y], fin.at[c, y], q5_s.at[c, i - 1], q5_r.at[c, i - 1], yp[i - 1])

    def along_z_hi_first(c):
        got(r4.at[c, 1], q4_r.at[c, 0])
        r4[c, 2] = (r4[c, 0].astype(F32) + r4[c, 1].astype(F32)).astype(BF16)
        to = pick(jnp.logical_xor(rem(zh, 2) == 0, rem(c, 2) == 0), zp[0], zp[2])
        send(r4.at[c, 2], r4.at[c, 3], q4_s.at[c, 1], q4_r.at[c, 1], to)

    def along_z_hi(c):
        got(r4.at[c, 3], q4_r.at[c, 1])
        spread_y(c, r4[c, 2].astype(F32) + r4[c, 3].astype(F32))

    def along_z_hi_last(c):
        for i in range(1, NZH):
            got(r4.at[c, rem(zh + NZH - i, NZH)], q4_r.at[c, i - 1])
        total = r4[c, 0].astype(F32)
        for i in range(1, NZH):
            total = total + r4[c, i].astype(F32)
        spread_y(c, total)

    def back_y(c):
        for i in range(1, NY):
            got(fin.at[c, rem(y + NY - i, NY)], q5_r.at[c, i - 1])
        send(fin.at[c, 1 - k], gx.at[c], q6_s.at[c], q6_r.at[c], partner)
        go[k, c] = fin[c, k].astype(F32)
        second = fin[c, 2:4].reshape(R2, CW)
        rows = pl.ds(pl.multiple_of(HS * c, HS), HS)
        for n in range(NB):
            o_g2[rows, CW * n : CW * (n + 1)] = second[HS * n : HS * (n + 1), :].astype(F32)

    def out_rows(start, first, end):
        rows = pl.ds(pl.multiple_of(start, 256), 256)
        parts = []
        for n in range(NB):
            total = jnp.zeros((256, CW), F32)
            for c in range(first, end):
                total = total + jnp.dot(hid[c, rows, :], second_of(c, n), preferred_element_type=F32)
            parts.append(total)
        return jnp.concatenate(parts, axis=1)

    def back_rows(start, first, end):
        rows = pl.ds(pl.multiple_of(start, 256), 256)
        total = jnp.zeros((256, D), F32)
        for c in range(first, end):
            total = total + lax.dot_general(
                bb[c, rows, :], first_of(c), (((1,), (1,)), ((), ())), preferred_element_type=F32
            )
        return total

    def tail_out(first, end):
        def step(m, carry):
            m = lax.rem(m + 2 * (1 - k), 4)
            rows = pl.ds(pl.multiple_of(256 * m, 256), 256)
            mixed, back = out_rows(256 * m, first, end), back_rows(256 * m, first, end)
            if first > 0:
                mixed, back = mixed + po[rows, :], back + pb[rows, :]
            po[rows, :] = mixed
            pb[rows, :] = back
            return carry

        if first == 0:
            lax.fori_loop(0, 4, step, 0)
            return
        lax.fori_loop(0, 2, step, 0)
        px[0] = po[there, :].astype(BF16)
        px[1] = pb[there, :].astype(BF16)
        for i in range(2):
            send(px.at[i], rx.at[i], p_s.at[i], p_r.at[i], partner)
        lax.fori_loop(2, 4, step, 0)

    def tail_rows():
        for i in range(2):
            got(rx.at[i], p_r.at[i])

        def step(m, carry):
            rows = pl.ds(pl.multiple_of(128 * m, 128), 128)
            at = pl.ds(pl.multiple_of(ROWS * k + 128 * m, 128), 128)
            live = flag_s[rows, :][:, 0:1] > 0
            plain = tok[rows, :].astype(F32)
            mixed = plain + (po[at, :] + rx[0, rows, :].astype(F32))
            o_out[rows, :] = jnp.where(live, mixed, plain).astype(BF16)
            normed = nf[at, :]
            inverse = inv_s[at, :][:, 0:1]
            back = pb[at, :] + rx[1, rows, :].astype(F32)
            scaled = back * gains
            first = jnp.mean(scaled, axis=1, keepdims=True)
            second = jnp.mean(scaled * normed, axis=1, keepdims=True)
            upstream = cot[rows, :].astype(F32)
            value = upstream + inverse * (scaled - first - normed * second)
            o_grad[rows, :] = jnp.where(live, value, upstream).astype(BF16)
            return carry

        lax.fori_loop(0, 4, step, 0)

    def gain_core():
        row = gacc[...] * SCALE / gains
        tile = jnp.zeros((8, 128), F32)
        line = lax.broadcasted_iota(jnp.int32, (8, 128), 0)
        for qs in range(8):
            turned = (pltpu.roll(row, D - 96 * qs, 1) if qs else row)[:, 0:128]
            tile = jnp.where(line == qs, turned, tile)
        gz[0] = tile
        send(gz.at[0], gz.at[1], a_s.at[0], a_r.at[0], partner)

    def gain_z_lo():
        got(gz.at[1], a_r.at[0])
        gz[2] = gz[0] + gz[1]
        send(gz.at[2], gz.at[3], a_s.at[1], a_r.at[1], near)

    def gain_x():
        got(gz.at[3], a_r.at[1])
        gxx[x] = gz[2] + gz[3]
        for i in range(1, NX):
            send(gxx.at[x], gxx.at[x], a_s.at[1 + i], a_r.at[1 + i], xp[i - 1])

    def gain_y():
        for i in range(1, NX):
            got(gxx.at[rem(x + NX - i, NX)], a_r.at[1 + i])
        gyy[y] = gxx[0] + gxx[1] + gxx[2] + gxx[3]
        for i in range(1, NY):
            send(gyy.at[y], gyy.at[y], a_s.at[4 + i], a_r.at[4 + i], yp[i - 1])

    def gain_z_hi():
        for i in range(1, NY):
            got(gyy.at[rem(y + NY - i, NY)], a_r.at[4 + i])
        gzz[zh] = gyy[0] + gyy[1] + gyy[2] + gyy[3]
        for i in range(1, NZH):
            send(gzz.at[zh], gzz.at[zh], a_s.at[7 + i], a_r.at[7 + i], zp[i - 1])

    def gain_last():
        for i in range(1, NZH):
            got(gzz.at[rem(zh + NZH - i, NZH)], a_r.at[7 + i])
        total = gzz[0] + gzz[1] + gzz[2] + gzz[3]
        line = lax.broadcasted_iota(jnp.int32, (8, 128), 0)
        row = jnp.sum(jnp.where(line == q, total, 0.0), axis=0, keepdims=True)
        row = jnp.broadcast_to(row, (8, 128))
        row = jnp.where(k == 1, pltpu.roll(row, 80, 1), row)
        o_gain[...] = row[0:1, 0:48]

    def gather_core(c):
        if c in taken:
            return
        taken.add(c)
        got(gx.at[c], q6_r.at[c])
        go[1 - k, c] = gx[c].astype(F32)

    taken = set()

    def drain(late):
        def each(first, end, work):
            def step(c, carry):
                work(c)
                return carry

            lax.fori_loop(first, end, step, 0)

        def weights(c):
            for i in range(NX - 1):
                got(wg.at[c, zl, x, my_half], ag_s.at[c, i])
            for i in range(2):
                got(wg.at[c, zl, 0:2, my_half], az_s.at[c, i])
                got(r1.at[c, 0:2], q1_s.at[c, i])
            for i in range(4):
                got(wg.at[c, zl, 0:2, my_half], ay_s.at[c, i])

        def by_x(c):
            for i in range(3):
                got(r2.at[c, i], q2_s.at[c, i])

        def by_y(c):
            for i in range(3):
                got(r3.at[c, i], q3_s.at[c, i])

        def by_z_hi(c):
            for i in range(2):
                got(r4.at[c, 0], q4_s.at[c, i])

        def by_back(c):
            for i in range(3):
                got(fin.at[c, y], q5_s.at[c, i])
            got(gx.at[c], q6_s.at[c])

        if not late:
            each(0, C, weights)
            each(0, C - 1, by_x)
            each(0, C - 2, by_y)
            each(0, C - 4, by_z_hi)

            @pl.when(jnp.logical_not(y_odd))
            def _():
                got(wg.at[:, zl, x, mine, :], w_s)

            for i in range(2):
                got(tk.at[here], t_s.at[i])
                got(px.at[i], p_s.at[i])
            for i in range(4):
                got(gsum.at[0], gg_s.at[i])
            got(gt.at[zl], gg_s.at[4])
            return
        by_x(C - 1)
        each(C - 2, C, by_y)
        each(C - 4, C, by_z_hi)
        got(r4.at[C - 1, 0], q4_s.at[C - 1, 2])
        each(0, C, by_back)
        for i in range(11):
            got(gz.at[0], a_s.at[i])

    def slot(t, carry):
        @pl.when(t + 2 < C)
        def _():
            forward_x(t + 2)

        @pl.when(t + 3 < C)
        def _():
            first_sends(t + 3)

        @pl.when(t + 1 < C)
        def _():
            forward_z(t + 1)

        @pl.when(t < C)
        def _():
            grads(t)

        @pl.when(t == SPLIT)
        def _():
            tail_out(0, SPLIT)

        for late, work in ((1, along_z_lo), (2, along_x), (3, along_y), (4, along_z_hi_first), (5, along_z_hi), (6, back_y)):

            @pl.when(jnp.logical_and(t >= late, t < C + late))
            def _():
                work(t - late)

        return carry

    lax.fori_loop(0, C, slot, 0)
    gain_core()
    tail_out(SPLIT, C)
    along_x(C - 2)
    along_z_lo(C - 1)
    gain_z_lo()
    along_y(C - 3)
    along_z_hi_first(C - 4)
    along_z_hi(C - 5)
    back_y(C - 6)
    tail_rows()
    drain(late=False)
    along_x(C - 1)
    gain_x()
    along_y(C - 2)
    along_z_hi_first(C - 3)
    along_z_hi(C - 4)
    back_y(C - 5)
    gather_core(0)
    along_y(C - 1, last=True)
    gain_y()
    along_z_hi_first(C - 2)
    along_z_hi(C - 3)
    back_y(C - 4)
    gather_core(1)
    along_z_hi_last(C - 1)
    gain_z_hi()
    along_z_hi(C - 2)
    back_y(C - 3)
    gather_core(2)
    back_y(C - 2)
    gain_last()
    gather_core(3)
    back_y(C - 1)

    drain(late=True)
    for c in range(C):
        gather_core(c)
    place = {}
    for core in range(2):
        for c in range(C):
            for qs in range(8):
                place[hidden_block(core, c, qs)] = (core, c, qs)
    for block in range(H // 128):
        pieces = []
        for i in range(per):
            core, c, qs = place[per * block + i]
            start = qs // per * 128
            pieces.append((go[core, c, :, start : start + 128], qs % per))
        o_g1[:, 128 * block : 128 * (block + 1)] = gather_lanes(pieces)


def place_kernel(*refs):
    count = len(refs) // 2
    for i in range(count):
        refs[count + i][...] = refs[i][...]


def body(tokens, cotangent, live_index, live_count, norm_gain, w_first, w_second):
    images, patches, width = tokens.shape
    tok, cot = tokens.reshape(ROWS, D), cotangent.reshape(ROWS, D)
    vmem = pl.BlockSpec(memory_space=pltpu.VMEM)
    smem = pl.BlockSpec(memory_space=pltpu.SMEM)
    dma = pltpu.SemaphoreType.DMA
    scratch = [
        pltpu.VMEM((2, C, R1 // 2, CW), BF16),
        pltpu.VMEM((C, 2, NX, SR, CW), BF16),
        pltpu.VMEM((2 * ROWS, D), BF16),
        pltpu.VMEM((2 * ROWS, D), BF16),
        pltpu.VMEM((2 * ROWS, D), BF16),
        pltpu.VMEM((D, 2 * ROWS), BF16),
        pltpu.VMEM((2 * ROWS, D), F32),
        pltpu.VMEM((2 * ROWS, 128), F32),
        pltpu.VMEM((ROWS, 128), F32),
        pltpu.VMEM((C, 2 * ROWS, CW), BF16),
        pltpu.VMEM((C, 2 * ROWS, CW), BF16),
        pltpu.VMEM((C, 2, NX, SR, CW), BF16),
        pltpu.VMEM((C, NX, SR, CW), BF16),
        pltpu.VMEM((C, NX, SR, CW), BF16),
        pltpu.VMEM((C, NX - 1, SR, CW), BF16),
        pltpu.VMEM((C, SR, CW), BF16),
        pltpu.VMEM((C, NY - 1, PR, CW), BF16),
        pltpu.VMEM((C, NZH, PR, CW), BF16),
        pltpu.VMEM((C, NY, PR, CW), BF16),
        pltpu.VMEM((C, PR, CW), BF16),
        pltpu.VMEM((2, C, R1 // 2, CW), F32),
        pltpu.VMEM((2 * ROWS, D), F32),
        pltpu.VMEM((2 * ROWS, D), F32),
        pltpu.VMEM((2, ROWS, D), BF16),
        pltpu.VMEM((2, ROWS, D), BF16),
        pltpu.VMEM((2, NX, 8, 128), F32),
        pltpu.VMEM((4, 8, 128), F32),
        pltpu.VMEM((8, D), F32),
        pltpu.VMEM((4, 8, 128), F32),
        pltpu.VMEM((4, 8, 128), F32),
        pltpu.VMEM((4, 8, 128), F32),
        pltpu.VMEM((4, 8, 128), F32),
        dma((C, 3)), dma((C, 3)),
        dma((C, 2)), dma((C, 2)),
        dma((C, 4)), dma((C, 4)),
        dma((C, 2)), dma((C, 2)),
        dma((C, 3)), dma((C, 3)),
        dma((C, 3)), dma((C, 3)),
        dma((C, 3)), dma((C, 3)),
        dma((C, 3)), dma((C, 3)),
        dma((C,)), dma((C,)),
        dma, dma,
        dma((2,)), dma((2,)),
        dma((5,)), dma((5,)),
        dma((2,)), dma((2,)),
        dma((11,)), dma((11,)),
    ]
    out, grad, g1, g2, gg = pl.pallas_call(
        kernel,
        out_shape=(
            jax.ShapeDtypeStruct((ROWS, D), BF16),
            jax.ShapeDtypeStruct((ROWS, D), BF16),
            jax.ShapeDtypeStruct((48, H), F32),
            jax.ShapeDtypeStruct((192, D), F32),
            jax.ShapeDtypeStruct((1, 48), F32),
        ),
        in_specs=[vmem, vmem, vmem, smem, vmem, vmem, vmem],
        out_specs=(vmem,) * 5,
        scratch_shapes=scratch,
        compiler_params=pltpu.CompilerParams(
            collective_id=0, has_side_effects=True, vmem_limit_bytes=60 << 20
        ),
        cost_estimate=pl.CostEstimate(flops=14 * 10**9, bytes_accessed=10**7, transcendentals=0),
    )(tok, cot, live_index, live_count, norm_gain.reshape(1, 48), w_first, w_second)
    made = (out, grad, g1, g2, gg)
    out, grad, g1, g2, gg = pl.pallas_call(
        place_kernel,
        out_shape=tuple(jax.ShapeDtypeStruct(v.shape, v.dtype) for v in made),
        in_specs=[vmem] * 5,
        out_specs=(vmem,) * 5,
    )(*made)
    return (
        out.reshape(images, patches, width),
        grad.reshape(images, patches, width),
        g1,
        g2,
        gg.reshape(48),
    )


def solution(mesh):
    return jax.shard_map(
        body,
        mesh=mesh,
        in_specs=(
            P(("dp", "fsdp"), None, None),
            P(("dp", "fsdp"), None, None),
            P(("dp", "fsdp"), None),
            P(("dp", "fsdp")),
            P("fsdp"),
            P("fsdp", None),
            P("fsdp", None),
        ),
        out_specs=(
            P(("dp", "fsdp"), None, None),
            P(("dp", "fsdp"), None, None),
            P("fsdp", None),
            P("fsdp", None),
            P("fsdp"),
        ),
        check_vma=False,
    )
```

```python
import functools

import jax
import jax.numpy as jnp
from jax import lax
from jax.experimental import pallas as pl
from jax.experimental.pallas import tpu as pltpu
from jax.sharding import PartitionSpec as P

epsilon = 1e-06
root_two_pi = 0.7978845608028654
cubic = 0.044715

MESH = pl.DeviceIdType.MESH
NX, NY, NZH = 4, 4, 4
D, H, ROWS, PATCHES = 768, 3072, 512, 256
SPLIT = 4
GROUPS = ((0, 3), (3, 5), (5, 6))
LAST = 2
C = 6
HS = 192 // C
CW = 8 * HS
R1, R2 = D // 8, D * HS // CW
NB = D // CW
SR = R1 + R2
PR = SR // NY
SCALE = 1.0 / PATCHES
F32, BF16 = jnp.float32, jnp.bfloat16


def rem(a, n):
    return lax.rem(a, jnp.int32(n))


def kernel(tok, cot, idx, cnt, gain, w_in, w2, o_out, o_grad, o_g1, o_g2, o_gain,
           w1, wg, tk, ct, nrm, nt, nf, inv_s, flag_s, hid, bb, buf, r1, s1, r2, s2, r3, r4, fin, gx,
           go, po, pb, px, rx, gt, gsum, gacc, gz, gxx, gyy, gzz,
           ag_s, ag_r, az_s, az_r, ay_s, ay_r, q1_s, q1_r, q2_s, q2_r, q3_s, q3_r, q4_s, q4l_s, q4_r, q5_s, q5_r, q6_s, q6_r,
           w_s, w_r, t_s, t_r, gg_s, gg_r, p_s, p_r, a_s, a_r):
    dp, f = lax.axis_index("dp"), lax.axis_index("fsdp")
    x, zl, k = lax.div(f, jnp.int32(4)), rem(lax.div(f, jnp.int32(2)), 2), rem(f, 2)
    zh, y = lax.div(dp, jnp.int32(4)), rem(dp, 4)
    z, q = zh * 2 + zl, lax.div(f, jnp.int32(2))

    def dev(x_, y_, z_, k_):
        return (lax.div(z_, jnp.int32(2)) * 4 + y_, x_ * 4 + rem(z_, 2) * 2 + k_)

    z_near = zh * 2 + (1 - zl)
    z_far = rem(z + 8 + 2 * zl - 1, 8)
    partner = dev(x, y, z, 1 - k)
    near, far = dev(x, y, z_near, k), dev(x, y, z_far, k)
    xp = [dev(rem(x + i, NX), y, z, k) for i in range(1, NX)]
    yp = [dev(x, rem(y + i, NY), z, k) for i in range(1, NY)]
    zp = [dev(x, y, rem(z + 2 * i, 8), k) for i in range(1, NZH)]

    def send(src, dst, s_sem, r_sem, to):
        copy = pltpu.make_async_remote_copy(
            src_ref=src, dst_ref=dst, send_sem=s_sem, recv_sem=r_sem, device_id=to, device_id_type=MESH
        )
        copy.start()

    def got(ref, sem):
        pltpu.make_async_copy(ref, ref, sem).wait()

    everyone = [partner, near, far] + xp + yp + zp
    barrier = pltpu.get_barrier_semaphore()
    for peer in everyone:
        pl.semaphore_signal(barrier, inc=1, device_id=peer, device_id_type=MESH)

    lane = lax.broadcasted_iota(jnp.int32, (R1 // 2, 128), 1)
    per = 128 // HS

    def gather_lanes(pieces):
        block = None
        for i, (value, at) in enumerate(pieces):
            turned = value if at == i else pltpu.roll(value, (i - at) * HS % 128, 1)
            block = turned if block is None else jnp.where(lane >= HS * i, turned, block)
        return block

    def hidden_block(core, c, qs):
        return (2 * qs + core) * C + c

    gains_own = jnp.broadcast_to(gain[...].astype(F32), (8, 48))
    gsum[0] = jnp.zeros((8, 128), F32)
    for core in range(2):

        @pl.when(k == core)
        def _():
            gsum[0, :, 48 * core : 48 * (core + 1)] = gains_own

    gacc[...] = jnp.zeros((8, D), F32)
    y_odd = rem(y, 2) == 1

    @pl.when(jnp.logical_not(y_odd))
    def _():
        for core in range(2):
            for c in range(C):
                for part in range(CW // 128):
                    pieces = []
                    for i in range(per):
                        block = hidden_block(core, c, per * part + i)
                        start = block // per * 128
                        pieces.append((w_in[:, start : start + 128].astype(F32), block % per))
                    w1[core, c, :, 128 * part : 128 * (part + 1)] = gather_lanes(pieces).astype(BF16)

    @pl.when(y_odd)
    def _():
        for c in range(C):
            for n in range(NB):
                wg[c, zl, x, R1 + HS * n : R1 + HS * (n + 1), :] = w2[
                    HS * c : HS * (c + 1), CW * n : CW * (n + 1)
                ]

    pl.semaphore_wait(barrier, len(everyone))

    send(gsum.at[0], gsum.at[1], gg_s, gg_r.at[0], partner)
    mine = pl.ds(pl.multiple_of(R1 // 2 * k, 16), R1 // 2)
    other = pl.ds(pl.multiple_of(R1 // 2 * (1 - k), 16), R1 // 2)

    @pl.when(jnp.logical_not(y_odd))
    def _():
        send(w1.at[1 - k], wg.at[:, zl, x, mine, :], w_s, w_r, partner)
        for c in range(C):
            wg[c, zl, x, mine, :] = w1[k, c]
        got(wg.at[:, zl, x, other, :], w_r)

    half = rem(y, 2)
    my_half = pl.ds(pl.multiple_of(SR // 2 * half, 16), SR // 2)
    its_half = pl.ds(pl.multiple_of(SR // 2 * (1 - half), 16), SR // 2)

    def pick(cond, a, b):
        return tuple(jnp.where(cond, i, j) for i, j in zip(a, b))

    def first_sends(c):
        block = wg.at[c, zl, x, my_half]
        for i in range(1, NX):
            send(block, block, ag_s, ag_r.at[c], xp[i - 1])

    first_sends(0)

    got(gsum.at[1], gg_r.at[0])
    gt[zl, x] = gsum[0] + gsum[1]
    for i in range(1, NX):
        send(gt.at[zl, x], gt.at[zl, x], gg_s, gg_r.at[i], xp[i - 1])

    for image in range(2):
        at = lax.broadcasted_iota(jnp.int32, (PATCHES, PATCHES), 0)
        place = lax.broadcasted_iota(jnp.int32, (PATCHES, PATCHES), 1)
        hit = jnp.where(
            jnp.logical_and(idx[image : image + 1, :] == at, place < cnt[image]), 1.0, 0.0
        ).astype(F32)
        flag = jnp.max(hit, axis=1, keepdims=True)
        rows = slice(PATCHES * image, PATCHES * (image + 1))
        flag_s[rows, :] = jnp.broadcast_to(flag, (PATCHES, 128))
        to = pl.ds(pl.multiple_of(ROWS * k + PATCHES * image, PATCHES), PATCHES)
        tk[to, :] = jnp.where(flag > 0, tok[rows, :].astype(F32), 0.0).astype(BF16)
        ct[to, :] = jnp.where(flag > 0, cot[rows, :].astype(F32), 0.0).astype(BF16)
    here = pl.ds(pl.multiple_of(ROWS * k, ROWS), ROWS)
    there = pl.ds(pl.multiple_of(ROWS * (1 - k), ROWS), ROWS)
    send(tk.at[here], tk.at[here], t_s, t_r, partner)
    send(ct.at[here], ct.at[here], t_s, t_r, partner)

    def swap(c, kind, spread, to):
        if spread:
            for i, ends in enumerate((yp[0], yp[2])):
                block = wg.at[c, kind, 2 * i : 2 * i + 2, my_half]
                send(block, block, ay_s, ay_r.at[c], ends)
        else:
            block = wg.at[c, kind, :, my_half]
            send(block, block, ay_s, ay_r.at[c], to)

    def forward_x(c, spread=False):
        got(wg.at[c, zl, 0 : NX - 1, my_half], ag_r.at[c])
        for i, to in enumerate((near, far)):
            block = wg.at[c, zl, 2 * i : 2 * i + 2, my_half]
            send(block, block, az_s, az_r.at[c], to)
        swap(c, zl, spread, yp[0])

    def forward_z(c, spread=False):
        got(wg.at[c, 1 - zl, :, my_half], az_r.at[c])
        swap(c, 1 - zl, spread, yp[2])

    for i in range(1, NX):
        got(gt.at[zl, rem(x + NX - i, NX)], gg_r.at[i])
    send(gt.at[zl], gt.at[zl], gg_s, gg_r.at[4], near)
    forward_x(0, spread=True)
    first_sends(1)
    got(gt.at[1 - zl], gg_r.at[4])
    got(tk, t_r)

    def gain_row():
        total = jnp.zeros((8, D), F32)
        for qs in range(8):
            tile = jnp.concatenate([gt[qs % 2, qs // 2], jnp.zeros((8, D - 128), F32)], axis=1)
            total = total + (pltpu.roll(tile, 96 * qs, 1) if qs else tile)
        return total[0:1, :]

    gains = gain_row()

    def norm_step(m, carry):
        rows = pl.ds(pl.multiple_of(256 * m, 256), 256)
        values = tk[rows, :].astype(F32)
        center = jnp.mean(values, axis=1, keepdims=True)
        values = values - center
        spread = jnp.mean(values * values, axis=1, keepdims=True)
        inverse = lax.rsqrt(spread + epsilon)
        normed = values * inverse
        nf[rows, :] = normed
        inv_s[rows, :] = jnp.broadcast_to(inverse, (256, 128))
        normal = normed * gains
        nrm[rows, :] = normal.astype(BF16)
        nt[:, rows] = jnp.transpose(normal).astype(BF16)
        return carry

    lax.fori_loop(0, 4, norm_step, 0)
    forward_z(0, spread=True)
    forward_x(1)
    first_sends(2)

    def first_of(c):
        return jnp.concatenate([wg[c, qs % 2, qs // 2, 0:R1, :] for qs in range(8)], axis=0)

    def second_of(c, n):
        rows = slice(R1 + HS * n, R1 + HS * (n + 1))
        return jnp.concatenate([wg[c, qs % 2, qs // 2, rows, :] for qs in range(8)], axis=0)

    def grads(c):
        got(wg.at[c, :, :, its_half], ay_r.at[c])

        def step(m, carry):
            rows = pl.ds(pl.multiple_of(256 * m, 256), 256)
            before = jnp.dot(nrm[rows, :], first_of(c), preferred_element_type=F32)
            back = jnp.zeros((256, CW), F32)
            for n in range(NB):
                back = back + lax.dot_general(
                    ct[rows, CW * n : CW * (n + 1)], second_of(c, n), (((1,), (1,)), ((), ())),
                    preferred_element_type=F32,
                )
            square = before * before
            tangent = jnp.tanh(before * (root_two_pi + (root_two_pi * cubic) * square))
            half = 0.5 + 0.5 * tangent
            hid[c, rows, :] = (before * half).astype(BF16)
            slope = half + (0.5 * before) * (1.0 - tangent * tangent) * (
                root_two_pi + (3.0 * cubic * root_two_pi) * square
            )
            bb[c, rows, :] = (back * slope).astype(BF16)
            return carry

        lax.fori_loop(0, 4, step, 0, unroll=True)
        for part in range(2):
            term = jnp.dot(nt[384 * part : 384 * (part + 1), :], bb[c], preferred_element_type=F32)
            own_rows = jnp.concatenate(
                [wg[c, qs % 2, qs // 2, 0:R1, :] for qs in range(4 * part, 4 * part + 4)], axis=0
            )
            product = term * own_rows.astype(F32)
            high = product.astype(BF16)
            low = (product - high.astype(F32)).astype(BF16)
            ones = jnp.ones((8, CW), BF16)
            line_sum = jnp.zeros((8, 384), F32)
            for share in (high, low):
                line_sum = line_sum + lax.dot_general(
                    ones, share, (((1,), (1,)), ((), ())), preferred_element_type=F32
                )
            gacc[:, 384 * part : 384 * (part + 1)] += line_sum
            term = (term * SCALE).astype(BF16)
            for i in range(4):
                qs = 4 * part + i
                buf[c, qs % 2, qs // 2, 0:R1, :] = term[R1 * i : R1 * (i + 1), :]
        for n in range(NB):
            term = lax.dot_general(
                hid[c], ct[:, CW * n : CW * (n + 1)], (((0,), (0,)), ((), ())), preferred_element_type=F32
            )
            term = (term * SCALE).astype(BF16)
            for qs in range(8):
                buf[c, qs % 2, qs // 2, R1 + HS * n : R1 + HS * (n + 1), :] = term[HS * qs : HS * (qs + 1), :]
        send(buf.at[c, 1 - zl, 0:2], r1.at[c, 0:2], q1_s, q1_r.at[c], near)
        send(buf.at[c, 1 - zl, 2:4], r1.at[c, 2:4], q1_s, q1_r.at[c], far)

    def along_z_lo(c):
        got(r1.at[c], q1_r.at[c])
        for i in range(NX):
            s1[c, i] = (buf[c, zl, i].astype(F32) + r1[c, i].astype(F32)).astype(BF16)
        for i in range(1, NX):
            send(s1.at[c, rem(x + i, NX)], r2.at[c, i - 1], q2_s, q2_r.at[c], xp[i - 1])

    def along_x(c):
        got(r2.at[c], q2_r.at[c])
        total = s1[c, x].astype(F32)
        for i in range(NX - 1):
            total = total + r2[c, i].astype(F32)
        s2[c] = total.astype(BF16)

    def start_y(g):
        first, end = GROUPS[g]
        for i in range(1, NY):
            part = pl.ds(pl.multiple_of(PR * rem(y + i, NY), 16), PR)
            send(s2.at[first:end, part], r3.at[i - 1, first:end], q3_s, q3_r.at[g], yp[i - 1])

    def along_y(g):
        first, end = GROUPS[g]
        got(r3.at[:, first:end], q3_r.at[g])
        total = s2[first:end, pl.ds(pl.multiple_of(PR * y, 16), PR), :].astype(F32)
        for i in range(NY - 1):
            total = total + r3[i, first:end].astype(F32)
        if g == LAST:
            r4[zh, first:end] = total.astype(BF16)
            for i in range(1, NZH):
                send(r4.at[zh, first:end], r4.at[zh, first:end], q4l_s, q4_r.at[g, 0], zp[i - 1])
        else:
            r4[0, first:end] = total.astype(BF16)
            to = pick(jnp.logical_xor(rem(zh, 2) == 0, g % 2 == 0), zp[2], zp[0])
            send(r4.at[0, first:end], r4.at[1, first:end], q4_s, q4_r.at[g, 0], to)

    def spread_y(g, total):
        first, end = GROUPS[g]
        fin[y, first:end] = total.astype(BF16)
        for i in range(1, NY):
            send(fin.at[y, first:end], fin.at[y, first:end], q5_s, q5_r.at[g], yp[i - 1])

    def along_z_hi_first(g):
        first, end = GROUPS[g]
        got(r4.at[1, first:end], q4_r.at[g, 0])
        r4[2, first:end] = (r4[0, first:end].astype(F32) + r4[1, first:end].astype(F32)).astype(BF16)
        to = pick(jnp.logical_xor(rem(zh, 2) == 0, g % 2 == 0), zp[0], zp[2])
        send(r4.at[2, first:end], r4.at[3, first:end], q4_s, q4_r.at[g, 1], to)

    def along_z_hi(g):
        first, end = GROUPS[g]
        if g == LAST:
            got(r4.at[0 : NZH - 1, first:end], q4_r.at[g, 0])
            total = r4[0, first:end].astype(F32)
            for i in range(1, NZH):
                total = total + r4[i, first:end].astype(F32)
        else:
            got(r4.at[3, first:end], q4_r.at[g, 1])
            total = r4[2, first:end].astype(F32) + r4[3, first:end].astype(F32)
        spread_y(g, total)

    def back_y(g):
        first, end = GROUPS[g]
        got(fin.at[0 : NY - 1, first:end], q5_r.at[g])
        send(fin.at[1 - k, first:end], gx.at[first:end], q6_s, q6_r.at[g], partner)
        go[k, first:end] = fin[k, first:end].astype(F32)
        for c in range(first, end):
            second = fin[2:4, c].reshape(R2, CW).astype(F32)
            for n in range(NB):
                o_g2[HS * c : HS * (c + 1), CW * n : CW * (n + 1)] = second[HS * n : HS * (n + 1), :]

    def gather_core(g):
        first, end = GROUPS[g]
        got(gx.at[first:end], q6_r.at[g])
        go[1 - k, first:end] = gx[first:end].astype(F32)

    def out_rows(start, first, end):
        rows = pl.ds(pl.multiple_of(start, 256), 256)
        parts = []
        for n in range(NB):
            total = jnp.zeros((256, CW), F32)
            for c in range(first, end):
                total = total + jnp.dot(hid[c, rows, :], second_of(c, n), preferred_element_type=F32)
            parts.append(total)
        return jnp.concatenate(parts, axis=1)

    def back_rows(start, first, end):
        rows = pl.ds(pl.multiple_of(start, 256), 256)
        total = jnp.zeros((256, D), F32)
        for c in range(first, end):
            total = total + lax.dot_general(
                bb[c, rows, :], first_of(c), (((1,), (1,)), ((), ())), preferred_element_type=F32
            )
        return total

    def tail_out(first, end):
        def step(m, carry):
            m = lax.rem(m + 2 * (1 - k), 4)
            rows = pl.ds(pl.multiple_of(256 * m, 256), 256)
            mixed, back = out_rows(256 * m, first, end), back_rows(256 * m, first, end)
            if first > 0:
                mixed, back = mixed + po[rows, :], back + pb[rows, :]
            po[rows, :] = mixed
            pb[rows, :] = back
            return carry

        if first == 0:
            lax.fori_loop(0, 4, step, 0, unroll=True)
            return
        lax.fori_loop(0, 2, step, 0, unroll=True)
        px[0] = po[there, :].astype(BF16)
        px[1] = pb[there, :].astype(BF16)
        for i in range(2):
            send(px.at[i], rx.at[i], p_s, p_r, partner)
        lax.fori_loop(2, 4, step, 0, unroll=True)

    def tail_rows():
        got(rx, p_r)

        def step(m, carry):
            rows = pl.ds(pl.multiple_of(128 * m, 128), 128)
            at = pl.ds(pl.multiple_of(ROWS * k + 128 * m, 128), 128)
            live = flag_s[rows, :][:, 0:1] > 0
            plain = tok[rows, :].astype(F32)
            mixed = plain + (po[at, :] + rx[0, rows, :].astype(F32))
            o_out[rows, :] = jnp.where(live, mixed, plain).astype(BF16)
            normed = nf[at, :]
            inverse = inv_s[at, :][:, 0:1]
            back = pb[at, :] + rx[1, rows, :].astype(F32)
            scaled = back * gains
            first = jnp.mean(scaled, axis=1, keepdims=True)
            second = jnp.mean(scaled * normed, axis=1, keepdims=True)
            upstream = cot[rows, :].astype(F32)
            value = upstream + inverse * (scaled - first - normed * second)
            o_grad[rows, :] = jnp.where(live, value, upstream).astype(BF16)
            return carry

        lax.fori_loop(0, 4, step, 0)

    def gain_core():
        row = gacc[...] * SCALE / gains
        tile = jnp.zeros((8, 128), F32)
        line = lax.broadcasted_iota(jnp.int32, (8, 128), 0)
        for qs in range(8):
            turned = (pltpu.roll(row, D - 96 * qs, 1) if qs else row)[:, 0:128]
            tile = jnp.where(line == qs, turned, tile)
        gz[0] = tile
        send(gz.at[0], gz.at[1], a_s, a_r.at[0], partner)

    def gain_z_lo():
        got(gz.at[1], a_r.at[0])
        gz[2] = gz[0] + gz[1]
        send(gz.at[2], gz.at[3], a_s, a_r.at[1], near)

    def gain_x():
        got(gz.at[3], a_r.at[1])
        gxx[x] = gz[2] + gz[3]
        for i in range(1, NX):
            send(gxx.at[x], gxx.at[x], a_s, a_r.at[1 + i], xp[i - 1])

    def gain_y():
        for i in range(1, NX):
            got(gxx.at[rem(x + NX - i, NX)], a_r.at[1 + i])
        gyy[y] = gxx[0] + gxx[1] + gxx[2] + gxx[3]
        for i in range(1, NY):
            send(gyy.at[y], gyy.at[y], a_s, a_r.at[4 + i], yp[i - 1])

    def gain_z_hi():
        for i in range(1, NY):
            got(gyy.at[rem(y + NY - i, NY)], a_r.at[4 + i])
        gzz[zh] = gyy[0] + gyy[1] + gyy[2] + gyy[3]
        for i in range(1, NZH):
            send(gzz.at[zh], gzz.at[zh], a_s, a_r.at[7 + i], zp[i - 1])

    def gain_last():
        for i in range(1, NZH):
            got(gzz.at[rem(zh + NZH - i, NZH)], a_r.at[7 + i])
        total = gzz[0] + gzz[1] + gzz[2] + gzz[3]
        line = lax.broadcasted_iota(jnp.int32, (8, 128), 0)
        row = jnp.sum(jnp.where(line == q, total, 0.0), axis=0, keepdims=True)
        row = jnp.broadcast_to(row, (8, 128))
        row = jnp.where(k == 1, pltpu.roll(row, 80, 1), row)
        o_gain[...] = row[0:1, 0:48]

    def drain_first():
        got(r2.at[:, :, 0 : SR // 2], ag_s)
        got(wg.at[:, 0, :, 0 : SR // 2], az_s)
        got(wg.at[:, :, :, 0 : SR // 2], ay_s)
        got(r1, q1_s)
        got(tk, t_s)
        got(px, p_s)
        got(inv_s.at[0:64], gg_s)

        @pl.when(jnp.logical_not(y_odd))
        def _():
            got(wg.at[:, zl, x, mine, :], w_s)

    def drain_last():
        got(r2, q2_s)
        got(r3, q3_s)
        got(r4.at[0:2, 0 : GROUPS[LAST][0]], q4_s)
        got(r4.at[0 : NZH - 1, GROUPS[LAST][0] : C], q4l_s)
        got(fin.at[0 : NY - 1], q5_s)
        got(gx, q6_s)
        got(inv_s.at[0:88], a_s)

    def slot(t, carry):
        @pl.when(t + 2 < C)
        def _():
            forward_x(t + 2)

        @pl.when(t + 3 < C)
        def _():
            first_sends(t + 3)

        @pl.when(t + 1 < C)
        def _():
            forward_z(t + 1)

        @pl.when(t < C)
        def _():
            grads(t)

        @pl.when(t == SPLIT)
        def _():
            tail_out(0, SPLIT)

        for late, work in ((1, along_z_lo), (2, along_x)):

            @pl.when(t >= late)
            def _():
                work(t - late)

        @pl.when(t == GROUPS[0][1] + 1)
        def _():
            start_y(0)

        return carry

    lax.fori_loop(0, C, slot, 0)
    gain_core()
    tail_out(SPLIT, C)
    along_x(C - 2)
    start_y(1)
    along_y(0)
    along_z_lo(C - 1)
    gain_z_lo()
    tail_rows()
    along_z_hi_first(0)
    along_y(1)
    drain_first()
    along_x(C - 1)
    start_y(2)
    gain_x()
    along_z_hi(0)
    along_z_hi_first(1)
    along_y(2)
    gain_y()
    along_z_hi(1)
    back_y(0)
    along_z_hi(2)
    gain_z_hi()
    back_y(1)
    gather_core(0)
    gain_last()
    gather_core(1)
    back_y(2)
    drain_last()
    gather_core(2)
    place = {}
    for core in range(2):
        for c in range(C):
            for qs in range(8):
                place[hidden_block(core, c, qs)] = (core, c, qs)
    for block in range(H // 128):
        pieces = []
        for i in range(per):
            core, c, qs = place[per * block + i]
            start = qs // per * 128
            pieces.append((go[core, c, :, start : start + 128], qs % per))
        o_g1[:, 128 * block : 128 * (block + 1)] = gather_lanes(pieces)


def place_kernel(*refs):
    count = len(refs) // 2
    for i in range(count):
        refs[count + i][...] = refs[i][...]


def body(tokens, cotangent, live_index, live_count, norm_gain, w_first, w_second):
    images, patches, width = tokens.shape
    tok, cot = tokens.reshape(ROWS, D), cotangent.reshape(ROWS, D)
    vmem = pl.BlockSpec(memory_space=pltpu.VMEM)
    smem = pl.BlockSpec(memory_space=pltpu.SMEM)
    dma = pltpu.SemaphoreType.DMA
    scratch = [
        pltpu.VMEM((2, C, R1 // 2, CW), BF16),
        pltpu.VMEM((C, 2, NX, SR, CW), BF16),
        pltpu.VMEM((2 * ROWS, D), BF16),
        pltpu.VMEM((2 * ROWS, D), BF16),
        pltpu.VMEM((2 * ROWS, D), BF16),
        pltpu.VMEM((D, 2 * ROWS), BF16),
        pltpu.VMEM((2 * ROWS, D), F32),
        pltpu.VMEM((2 * ROWS, 128), F32),
        pltpu.VMEM((ROWS, 128), F32),
        pltpu.VMEM((C, 2 * ROWS, CW), BF16),
        pltpu.VMEM((C, 2 * ROWS, CW), BF16),
        pltpu.VMEM((C, 2, NX, SR, CW), BF16),
        pltpu.VMEM((C, NX, SR, CW), BF16),
        pltpu.VMEM((C, NX, SR, CW), BF16),
        pltpu.VMEM((C, NX - 1, SR, CW), BF16),
        pltpu.VMEM((C, SR, CW), BF16),
        pltpu.VMEM((NY - 1, C, PR, CW), BF16),
        pltpu.VMEM((NZH, C, PR, CW), BF16),
        pltpu.VMEM((NY, C, PR, CW), BF16),
        pltpu.VMEM((C, PR, CW), BF16),
        pltpu.VMEM((2, C, R1 // 2, CW), F32),
        pltpu.VMEM((2 * ROWS, D), F32),
        pltpu.VMEM((2 * ROWS, D), F32),
        pltpu.VMEM((2, ROWS, D), BF16),
        pltpu.VMEM((2, ROWS, D), BF16),
        pltpu.VMEM((2, NX, 8, 128), F32),
        pltpu.VMEM((4, 8, 128), F32),
        pltpu.VMEM((8, D), F32),
        pltpu.VMEM((4, 8, 128), F32),
        pltpu.VMEM((4, 8, 128), F32),
        pltpu.VMEM((4, 8, 128), F32),
        pltpu.VMEM((4, 8, 128), F32),
        dma, dma((C,)),
        dma, dma((C,)),
        dma, dma((C,)),
        dma, dma((C,)),
        dma, dma((C,)),
        dma, dma((3,)),
        dma, dma, dma((3, 2)),
        dma, dma((3,)),
        dma, dma((3,)),
        dma, dma,
        dma, dma,
        dma, dma((5,)),
        dma, dma,
        dma, dma((11,)),
    ]
    out, grad, g1, g2, gg = pl.pallas_call(
        kernel,
        out_shape=(
            jax.ShapeDtypeStruct((ROWS, D), BF16),
            jax.ShapeDtypeStruct((ROWS, D), BF16),
            jax.ShapeDtypeStruct((48, H), F32),
            jax.ShapeDtypeStruct((192, D), F32),
            jax.ShapeDtypeStruct((1, 48), F32),
        ),
        in_specs=[vmem, vmem, vmem, smem, vmem, vmem, vmem],
        out_specs=(vmem,) * 5,
        scratch_shapes=scratch,
        compiler_params=pltpu.CompilerParams(
            collective_id=0, has_side_effects=True, vmem_limit_bytes=60 << 20
        ),
        cost_estimate=pl.CostEstimate(flops=14 * 10**9, bytes_accessed=10**7, transcendentals=0),
    )(tok, cot, live_index, live_count, norm_gain.reshape(1, 48), w_first, w_second)
    made = (out, grad, g1, g2, gg)
    out, grad, g1, g2, gg = pl.pallas_call(
        place_kernel,
        out_shape=tuple(jax.ShapeDtypeStruct(v.shape, v.dtype) for v in made),
        in_specs=[vmem] * 5,
        out_specs=(vmem,) * 5,
    )(*made)
    return (
        out.reshape(images, patches, width),
        grad.reshape(images, patches, width),
        g1,
        g2,
        gg.reshape(48),
    )


def solution(mesh):
    return jax.shard_map(
        body,
        mesh=mesh,
        in_specs=(
            P(("dp", "fsdp"), None, None),
            P(("dp", "fsdp"), None, None),
            P(("dp", "fsdp"), None),
            P(("dp", "fsdp")),
            P("fsdp"),
            P("fsdp", None),
            P("fsdp", None),
        ),
        out_specs=(
            P(("dp", "fsdp"), None, None),
            P(("dp", "fsdp"), None, None),
            P("fsdp", None),
            P("fsdp", None),
            P("fsdp"),
        ),
        check_vma=False,
    )
```

```python
import functools

import jax
import jax.numpy as jnp
from jax import lax
from jax.experimental import pallas as pl
from jax.experimental.pallas import tpu as pltpu
from jax.sharding import PartitionSpec as P

epsilon = 1e-06
root_two_pi = 0.7978845608028654
cubic = 0.044715

MESH = pl.DeviceIdType.MESH
NX, NY, NZH = 4, 4, 4
D, H, ROWS, PATCHES = 768, 3072, 512, 256
SPLIT = 4
GROUPS = ((0, 2), (2, 4), (4, 5))
C = 6
HS = 192 // C
CW = 8 * HS
R1, R2 = D // 8, D * HS // CW
NB = D // CW
SR = R1 + R2
PR = SR // NY
SCALE = 1.0 / PATCHES
F32, BF16 = jnp.float32, jnp.bfloat16


def rem(a, n):
    return lax.rem(a, jnp.int32(n))


def kernel(tok, cot, idx, cnt, gain, w_in, w2, o_out, o_grad, o_g1, o_g2, o_gain,
           w1, wg, tk, ct, nrm, nt, nf, inv_s, flag_s, hid, bb, buf, r1, s1, r2, s2, r3, r4, fin, gx,
           e1, eb, sl1, rl2, sl2, rl3, rl4, finl, xg, go, po, pb, px, rx, gt, gsum, gacc, gz, gxx, gyy, gzz,
           ag_s, ag_r, az_s, az_r, ay_s, ay_r, q1_s, q1_r, q2_s, q2_r, q3_s, q3_r, q4_s, q4_r, q5_s, q5_r, q6_s, q6_r,
           qe_r, qb_s, qb_r, l2_s, l2_r, l3_s, l3_r, l4_s, l4_r, l5_s, l5_r, l6_s, l6_r,
           w_s, w_r, t_s, t_r, gg_s, gg_r, p_s, p_r, a_s, a_r):
    dp, f = lax.axis_index("dp"), lax.axis_index("fsdp")
    x, zl, k = lax.div(f, jnp.int32(4)), rem(lax.div(f, jnp.int32(2)), 2), rem(f, 2)
    zh, y = lax.div(dp, jnp.int32(4)), rem(dp, 4)
    z, q = zh * 2 + zl, lax.div(f, jnp.int32(2))

    def dev(x_, y_, z_, k_):
        return (lax.div(z_, jnp.int32(2)) * 4 + y_, x_ * 4 + rem(z_, 2) * 2 + k_)

    z_near = zh * 2 + (1 - zl)
    z_far = rem(z + 8 + 2 * zl - 1, 8)
    partner = dev(x, y, z, 1 - k)
    near, far = dev(x, y, z_near, k), dev(x, y, z_far, k)
    xp = [dev(rem(x + i, NX), y, z, k) for i in range(1, NX)]
    yp = [dev(x, rem(y + i, NY), z, k) for i in range(1, NY)]
    zp = [dev(x, y, rem(z + 2 * i, 8), k) for i in range(1, NZH)]

    def send(src, dst, s_sem, r_sem, to):
        copy = pltpu.make_async_remote_copy(
            src_ref=src, dst_ref=dst, send_sem=s_sem, recv_sem=r_sem, device_id=to, device_id_type=MESH
        )
        copy.start()

    def got(ref, sem):
        pltpu.make_async_copy(ref, ref, sem).wait()

    near_other, far_other = dev(x, y, z_near, 1 - k), dev(x, y, z_far, 1 - k)
    everyone = [partner, near, far, near_other, far_other] + xp + yp + zp
    barrier = pltpu.get_barrier_semaphore()
    for peer in everyone:
        pl.semaphore_signal(barrier, inc=1, device_id=peer, device_id_type=MESH)

    lane = lax.broadcasted_iota(jnp.int32, (R1 // 2, 128), 1)
    per = 128 // HS

    def gather_lanes(pieces):
        block = None
        for i, (value, at) in enumerate(pieces):
            turned = value if at == i else pltpu.roll(value, (i - at) * HS % 128, 1)
            block = turned if block is None else jnp.where(lane >= HS * i, turned, block)
        return block

    def hidden_block(core, c, qs):
        return (2 * qs + core) * C + c

    gains_own = jnp.broadcast_to(gain[...].astype(F32), (8, 48))
    gsum[0] = jnp.zeros((8, 128), F32)
    for core in range(2):

        @pl.when(k == core)
        def _():
            gsum[0, :, 48 * core : 48 * (core + 1)] = gains_own

    gacc[...] = jnp.zeros((8, D), F32)
    y_odd = rem(y, 2) == 1

    @pl.when(jnp.logical_not(y_odd))
    def _():
        for core in range(2):
            for c in range(C):
                for part in range(CW // 128):
                    pieces = []
                    for i in range(per):
                        block = hidden_block(core, c, per * part + i)
                        start = block // per * 128
                        pieces.append((w_in[:, start : start + 128].astype(F32), block % per))
                    w1[core, c, :, 128 * part : 128 * (part + 1)] = gather_lanes(pieces).astype(BF16)

    @pl.when(y_odd)
    def _():
        for c in range(C):
            for n in range(NB):
                wg[c, zl, x, R1 + HS * n : R1 + HS * (n + 1), :] = w2[
                    HS * c : HS * (c + 1), CW * n : CW * (n + 1)
                ]

    pl.semaphore_wait(barrier, len(everyone))

    send(gsum.at[0], gsum.at[1], gg_s, gg_r.at[0], partner)
    mine = pl.ds(pl.multiple_of(R1 // 2 * k, 16), R1 // 2)
    other = pl.ds(pl.multiple_of(R1 // 2 * (1 - k), 16), R1 // 2)

    @pl.when(jnp.logical_not(y_odd))
    def _():
        send(w1.at[1 - k], wg.at[:, zl, x, mine, :], w_s, w_r, partner)
        for c in range(C):
            wg[c, zl, x, mine, :] = w1[k, c]
        got(wg.at[:, zl, x, other, :], w_r)

    half = rem(y, 2)
    my_half = pl.ds(pl.multiple_of(SR // 2 * half, 16), SR // 2)
    its_half = pl.ds(pl.multiple_of(SR // 2 * (1 - half), 16), SR // 2)

    def pick(cond, a, b):
        return tuple(jnp.where(cond, i, j) for i, j in zip(a, b))

    def first_sends(c):
        block = wg.at[c, zl, x, my_half]
        for i in range(1, NX):
            send(block, block, ag_s, ag_r.at[c], xp[i - 1])

    first_sends(0)

    got(gsum.at[1], gg_r.at[0])
    gt[zl, x] = gsum[0] + gsum[1]
    for i in range(1, NX):
        send(gt.at[zl, x], gt.at[zl, x], gg_s, gg_r.at[i], xp[i - 1])

    for image in range(2):
        at = lax.broadcasted_iota(jnp.int32, (PATCHES, PATCHES), 0)
        place = lax.broadcasted_iota(jnp.int32, (PATCHES, PATCHES), 1)
        hit = jnp.where(
            jnp.logical_and(idx[image : image + 1, :] == at, place < cnt[image]), 1.0, 0.0
        ).astype(F32)
        flag = jnp.max(hit, axis=1, keepdims=True)
        rows = slice(PATCHES * image, PATCHES * (image + 1))
        flag_s[rows, :] = jnp.broadcast_to(flag, (PATCHES, 128))
        to = pl.ds(pl.multiple_of(ROWS * k + PATCHES * image, PATCHES), PATCHES)
        tk[to, :] = jnp.where(flag > 0, tok[rows, :].astype(F32), 0.0).astype(BF16)
        ct[to, :] = jnp.where(flag > 0, cot[rows, :].astype(F32), 0.0).astype(BF16)
    here = pl.ds(pl.multiple_of(ROWS * k, ROWS), ROWS)
    there = pl.ds(pl.multiple_of(ROWS * (1 - k), ROWS), ROWS)
    send(tk.at[here], tk.at[here], t_s, t_r, partner)
    send(ct.at[here], ct.at[here], t_s, t_r, partner)

    def swap(c, kind, spread, to):
        if spread:
            for i, ends in enumerate((yp[0], yp[2])):
                block = wg.at[c, kind, 2 * i : 2 * i + 2, my_half]
                send(block, block, ay_s, ay_r.at[c], ends)
        else:
            block = wg.at[c, kind, :, my_half]
            send(block, block, ay_s, ay_r.at[c], to)

    def forward_x(c, spread=True):
        got(wg.at[c, zl, 0 : NX - 1, my_half], ag_r.at[c])
        for i, to in enumerate((near, far)):
            block = wg.at[c, zl, 2 * i : 2 * i + 2, my_half]
            send(block, block, az_s, az_r.at[c], to)
        swap(c, zl, spread, yp[0])

    def forward_z(c, spread=True):
        got(wg.at[c, 1 - zl, :, my_half], az_r.at[c])
        swap(c, 1 - zl, spread, yp[2])

    for i in range(1, NX):
        got(gt.at[zl, rem(x + NX - i, NX)], gg_r.at[i])
    send(gt.at[zl], gt.at[zl], gg_s, gg_r.at[4], near)
    forward_x(0, spread=True)
    first_sends(1)
    got(gt.at[1 - zl], gg_r.at[4])
    got(tk, t_r)

    def gain_row():
        total = jnp.zeros((8, D), F32)
        for qs in range(8):
            tile = jnp.concatenate([gt[qs % 2, qs // 2], jnp.zeros((8, D - 128), F32)], axis=1)
            total = total + (pltpu.roll(tile, 96 * qs, 1) if qs else tile)
        return total[0:1, :]

    gains = gain_row()

    def norm_step(m, carry):
        rows = pl.ds(pl.multiple_of(256 * m, 256), 256)
        values = tk[rows, :].astype(F32)
        center = jnp.mean(values, axis=1, keepdims=True)
        values = values - center
        spread = jnp.mean(values * values, axis=1, keepdims=True)
        inverse = lax.rsqrt(spread + epsilon)
        normed = values * inverse
        nf[rows, :] = normed
        inv_s[rows, :] = jnp.broadcast_to(inverse, (256, 128))
        normal = normed * gains
        nrm[rows, :] = normal.astype(BF16)
        nt[:, rows] = jnp.transpose(normal).astype(BF16)
        return carry

    lax.fori_loop(0, 4, norm_step, 0)
    forward_z(0, spread=True)
    forward_x(1)
    first_sends(2)

    def first_of(c):
        return jnp.concatenate([wg[c, qs % 2, qs // 2, 0:R1, :] for qs in range(8)], axis=0)

    def second_of(c, n):
        rows = slice(R1 + HS * n, R1 + HS * (n + 1))
        return jnp.concatenate([wg[c, qs % 2, qs // 2, rows, :] for qs in range(8)], axis=0)

    def grads(c):
        got(wg.at[c, :, :, its_half], ay_r.at[c])

        def step(m, carry):
            rows = pl.ds(pl.multiple_of(256 * m, 256), 256)
            before = jnp.dot(nrm[rows, :], first_of(c), preferred_element_type=F32)
            back = jnp.zeros((256, CW), F32)
            for n in range(NB):
                back = back + lax.dot_general(
                    ct[rows, CW * n : CW * (n + 1)], second_of(c, n), (((1,), (1,)), ((), ())),
                    preferred_element_type=F32,
                )
            square = before * before
            tangent = jnp.tanh(before * (root_two_pi + (root_two_pi * cubic) * square))
            half = 0.5 + 0.5 * tangent
            hid[c, rows, :] = (before * half).astype(BF16)
            slope = half + (0.5 * before) * (1.0 - tangent * tangent) * (
                root_two_pi + (3.0 * cubic * root_two_pi) * square
            )
            bb[c, rows, :] = (back * slope).astype(BF16)
            return carry

        lax.fori_loop(0, 4, step, 0, unroll=True)
        for part in range(2):
            term = jnp.dot(nt[384 * part : 384 * (part + 1), :], bb[c], preferred_element_type=F32)
            own_rows = jnp.concatenate(
                [wg[c, qs % 2, qs // 2, 0:R1, :] for qs in range(4 * part, 4 * part + 4)], axis=0
            )
            product = term * own_rows.astype(F32)
            high = product.astype(BF16)
            low = (product - high.astype(F32)).astype(BF16)
            ones = jnp.ones((8, CW), BF16)
            line_sum = jnp.zeros((8, 384), F32)
            for share in (high, low):
                line_sum = line_sum + lax.dot_general(
                    ones, share, (((1,), (1,)), ((), ())), preferred_element_type=F32
                )
            gacc[:, 384 * part : 384 * (part + 1)] += line_sum
            term = (term * SCALE).astype(BF16)
            for i in range(4):
                qs = 4 * part + i
                buf[c, qs % 2, qs // 2, 0:R1, :] = term[R1 * i : R1 * (i + 1), :]
        for n in range(NB):
            term = lax.dot_general(
                hid[c], ct[:, CW * n : CW * (n + 1)], (((0,), (0,)), ((), ())), preferred_element_type=F32
            )
            term = (term * SCALE).astype(BF16)
            for qs in range(8):
                buf[c, qs % 2, qs // 2, R1 + HS * n : R1 + HS * (n + 1), :] = term[HS * qs : HS * (qs + 1), :]
        to_odd = jnp.logical_and(c == C - 1, k == 0)

        @pl.when(jnp.logical_not(to_odd))
        def _():
            send(buf.at[c, 1 - zl, 0:2], r1.at[c, 0:2], q1_s, q1_r.at[c], near)
            send(buf.at[c, 1 - zl, 2:4], r1.at[c, 2:4], q1_s, q1_r.at[c], far)

        @pl.when(to_odd)
        def _():
            send(buf.at[c, 1 - zl, 0:2], e1.at[0:2], q1_s, qe_r, near_other)
            send(buf.at[c, 1 - zl, 2:4], e1.at[2:4], q1_s, qe_r, far_other)
            send(buf.at[c, zl], eb, qb_s, qb_r, partner)

    def along_z_lo(c):
        got(r1.at[c], q1_r.at[c])
        for i in range(NX):
            s1[c, i] = (buf[c, zl, i].astype(F32) + r1[c, i].astype(F32)).astype(BF16)
        for i in range(1, NX):
            send(s1.at[c, rem(x + i, NX)], r2.at[c, i - 1], q2_s, q2_r.at[c], xp[i - 1])

    def along_x(c):
        got(r2.at[c], q2_r.at[c])
        total = s1[c, x].astype(F32)
        for i in range(NX - 1):
            total = total + r2[c, i].astype(F32)
        s2[c] = total.astype(BF16)

    def start_y(g):
        first, end = GROUPS[g]
        for i in range(1, NY):
            part = pl.ds(pl.multiple_of(PR * rem(y + i, NY), 16), PR)
            send(s2.at[first:end, part], r3.at[i - 1, first:end], q3_s, q3_r.at[g], yp[i - 1])

    def along_y(g):
        first, end = GROUPS[g]
        got(r3.at[:, first:end], q3_r.at[g])
        total = s2[first:end, pl.ds(pl.multiple_of(PR * y, 16), PR), :].astype(F32)
        for i in range(NY - 1):
            total = total + r3[i, first:end].astype(F32)
        r4[0, first:end] = total.astype(BF16)
        to = pick(jnp.logical_xor(rem(zh, 2) == 0, g % 2 == 0), zp[2], zp[0])
        send(r4.at[0, first:end], r4.at[1, first:end], q4_s, q4_r.at[g, 0], to)

    def spread_y(g, total):
        first, end = GROUPS[g]
        fin[y, first:end] = total.astype(BF16)
        for i in range(1, NY):
            send(fin.at[y, first:end], fin.at[y, first:end], q5_s, q5_r.at[g], yp[i - 1])

    def along_z_hi_first(g):
        first, end = GROUPS[g]
        got(r4.at[1, first:end], q4_r.at[g, 0])
        r4[2, first:end] = (r4[0, first:end].astype(F32) + r4[1, first:end].astype(F32)).astype(BF16)
        to = pick(jnp.logical_xor(rem(zh, 2) == 0, g % 2 == 0), zp[0], zp[2])
        send(r4.at[2, first:end], r4.at[3, first:end], q4_s, q4_r.at[g, 1], to)

    def along_z_hi(g):
        first, end = GROUPS[g]
        got(r4.at[3, first:end], q4_r.at[g, 1])
        spread_y(g, r4[2, first:end].astype(F32) + r4[3, first:end].astype(F32))

    def put_second(c, parts):
        second = parts.reshape(R2, CW).astype(F32)
        for n in range(NB):
            o_g2[HS * c : HS * (c + 1), CW * n : CW * (n + 1)] = second[HS * n : HS * (n + 1), :]

    def back_y(g):
        first, end = GROUPS[g]
        got(fin.at[0 : NY - 1, first:end], q5_r.at[g])
        send(fin.at[1 - k, first:end], gx.at[first:end], q6_s, q6_r.at[g], partner)
        go[k, first:end] = fin[k, first:end].astype(F32)
        for c in range(first, end):
            put_second(c, fin[2:4, c])

    def gather_core(g):
        first, end = GROUPS[g]
        got(gx.at[first:end], q6_r.at[g])
        go[1 - k, first:end] = gx[first:end].astype(F32)

    def last_z():
        @pl.when(k == 1)
        def _():
            got(eb, qb_r)
            got(r1.at[C - 1], q1_r.at[C - 1])
            got(e1, qe_r)
            for i in range(NX):
                sl1[0, i] = (eb[i].astype(F32) + e1[i].astype(F32)).astype(BF16)
                sl1[1, i] = (buf[C - 1, zl, i].astype(F32) + r1[C - 1, i].astype(F32)).astype(BF16)
            for i in range(1, NX):
                send(sl1.at[:, rem(x + i, NX)], rl2.at[i - 1], l2_s, l2_r, xp[i - 1])

    def last_x():
        @pl.when(k == 1)
        def _():
            got(rl2, l2_r)
            total = sl1[:, x].astype(F32)
            for i in range(NX - 1):
                total = total + rl2[i].astype(F32)
            sl2[...] = total.astype(BF16)
            for i in range(1, NY):
                part = pl.ds(pl.multiple_of(PR * rem(y + i, NY), 16), PR)
                send(sl2.at[:, part], rl3.at[i - 1], l3_s, l3_r, yp[i - 1])

    def last_y():
        @pl.when(k == 1)
        def _():
            got(rl3, l3_r)
            total = sl2[:, pl.ds(pl.multiple_of(PR * y, 16), PR), :].astype(F32)
            for i in range(NY - 1):
                total = total + rl3[i].astype(F32)
            rl4[zh] = total.astype(BF16)
            for i in range(1, NZH):
                send(rl4.at[zh], rl4.at[zh], l4_s, l4_r, zp[i - 1])

    def last_z_hi():
        @pl.when(k == 1)
        def _():
            got(rl4.at[0 : NZH - 1], l4_r)
            total = rl4[0].astype(F32)
            for i in range(1, NZH):
                total = total + rl4[i].astype(F32)
            finl[y] = total.astype(BF16)
            for i in range(1, NY):
                send(finl.at[y], finl.at[y], l5_s, l5_r, yp[i - 1])

    def last_back():
        @pl.when(k == 1)
        def _():
            got(finl.at[0 : NY - 1], l5_r)
            send(finl.at[0], xg.at[0], l6_s, l6_r, partner)
            send(finl.at[2:4, 0], xg.at[1], l6_s, l6_r, partner)
            go[:, C - 1] = finl[1].astype(F32)
            put_second(C - 1, finl[2:4, 1])

    def last_take():
        @pl.when(k == 0)
        def _():
            got(xg, l6_r)
            go[:, C - 1] = xg[0].astype(F32)
            put_second(C - 1, xg[1])
            got(eb, qb_s)

        @pl.when(k == 1)
        def _():
            got(rl2, l2_s)
            got(rl3, l3_s)
            got(rl4.at[0 : NZH - 1], l4_s)
            got(finl.at[0 : NY - 1], l5_s)
            got(xg, l6_s)

    def out_rows(start, first, end):
        rows = pl.ds(pl.multiple_of(start, 256), 256)
        parts = []
        for n in range(NB):
            total = jnp.zeros((256, CW), F32)
            for c in range(first, end):
                total = total + jnp.dot(hid[c, rows, :], second_of(c, n), preferred_element_type=F32)
            parts.append(total)
        return jnp.concatenate(parts, axis=1)

    def back_rows(start, first, end):
        rows = pl.ds(pl.multiple_of(start, 256), 256)
        total = jnp.zeros((256, D), F32)
        for c in range(first, end):
            total = total + lax.dot_general(
                bb[c, rows, :], first_of(c), (((1,), (1,)), ((), ())), preferred_element_type=F32
            )
        return total

    def tail_out(first, end):
        def step(m, carry):
            m = lax.rem(m + 2 * (1 - k), 4)
            rows = pl.ds(pl.multiple_of(256 * m, 256), 256)
            mixed, back = out_rows(256 * m, first, end), back_rows(256 * m, first, end)
            if first > 0:
                mixed, back = mixed + po[rows, :], back + pb[rows, :]
            po[rows, :] = mixed
            pb[rows, :] = back
            return carry

        if first == 0:
            lax.fori_loop(0, 4, step, 0, unroll=True)
            return
        lax.fori_loop(0, 2, step, 0, unroll=True)
        px[0] = po[there, :].astype(BF16)
        px[1] = pb[there, :].astype(BF16)
        for i in range(2):
            send(px.at[i], rx.at[i], p_s, p_r, partner)
        lax.fori_loop(2, 4, step, 0, unroll=True)

    def tail_rows():
        got(rx, p_r)

        def step(m, carry):
            rows = pl.ds(pl.multiple_of(128 * m, 128), 128)
            at = pl.ds(pl.multiple_of(ROWS * k + 128 * m, 128), 128)
            live = flag_s[rows, :][:, 0:1] > 0
            plain = tok[rows, :].astype(F32)
            mixed = plain + (po[at, :] + rx[0, rows, :].astype(F32))
            o_out[rows, :] = jnp.where(live, mixed, plain).astype(BF16)
            normed = nf[at, :]
            inverse = inv_s[at, :][:, 0:1]
            back = pb[at, :] + rx[1, rows, :].astype(F32)
            scaled = back * gains
            first = jnp.mean(scaled, axis=1, keepdims=True)
            second = jnp.mean(scaled * normed, axis=1, keepdims=True)
            upstream = cot[rows, :].astype(F32)
            value = upstream + inverse * (scaled - first - normed * second)
            o_grad[rows, :] = jnp.where(live, value, upstream).astype(BF16)
            return carry

        lax.fori_loop(0, 4, step, 0)

    def gain_core():
        row = gacc[...] * SCALE / gains
        tile = jnp.zeros((8, 128), F32)
        line = lax.broadcasted_iota(jnp.int32, (8, 128), 0)
        for qs in range(8):
            turned = (pltpu.roll(row, D - 96 * qs, 1) if qs else row)[:, 0:128]
            tile = jnp.where(line == qs, turned, tile)
        gz[0] = tile
        send(gz.at[0], gz.at[1], a_s, a_r.at[0], partner)

    def gain_z_lo():
        got(gz.at[1], a_r.at[0])
        gz[2] = gz[0] + gz[1]
        send(gz.at[2], gz.at[3], a_s, a_r.at[1], near)

    def gain_x():
        got(gz.at[3], a_r.at[1])
        gxx[x] = gz[2] + gz[3]
        for i in range(1, NX):
            send(gxx.at[x], gxx.at[x], a_s, a_r.at[1 + i], xp[i - 1])

    def gain_y():
        for i in range(1, NX):
            got(gxx.at[rem(x + NX - i, NX)], a_r.at[1 + i])
        gyy[y] = gxx[0] + gxx[1] + gxx[2] + gxx[3]
        for i in range(1, NY):
            send(gyy.at[y], gyy.at[y], a_s, a_r.at[4 + i], yp[i - 1])

    def gain_z_hi():
        for i in range(1, NY):
            got(gyy.at[rem(y + NY - i, NY)], a_r.at[4 + i])
        gzz[zh] = gyy[0] + gyy[1] + gyy[2] + gyy[3]
        for i in range(1, NZH):
            send(gzz.at[zh], gzz.at[zh], a_s, a_r.at[7 + i], zp[i - 1])

    def gain_last():
        for i in range(1, NZH):
            got(gzz.at[rem(zh + NZH - i, NZH)], a_r.at[7 + i])
        total = gzz[0] + gzz[1] + gzz[2] + gzz[3]
        line = lax.broadcasted_iota(jnp.int32, (8, 128), 0)
        row = jnp.sum(jnp.where(line == q, total, 0.0), axis=0, keepdims=True)
        row = jnp.broadcast_to(row, (8, 128))
        row = jnp.where(k == 1, pltpu.roll(row, 80, 1), row)
        o_gain[...] = row[0:1, 0:48]

    def drain_first():
        got(r2.at[:, :, 0 : SR // 2], ag_s)
        got(wg.at[:, 0, :, 0 : SR // 2], az_s)
        got(wg.at[:, :, :, 0 : SR // 2], ay_s)
        got(r1, q1_s)
        got(tk, t_s)
        got(px, p_s)
        got(inv_s.at[0:64], gg_s)

        @pl.when(jnp.logical_not(y_odd))
        def _():
            got(wg.at[:, zl, x, mine, :], w_s)

    def drain_last():
        got(r2.at[0 : C - 1], q2_s)
        got(r3.at[:, 0 : C - 1], q3_s)
        got(r4.at[0:2, 0 : C - 1], q4_s)
        got(fin.at[0 : NY - 1, 0 : C - 1], q5_s)
        got(gx.at[0 : C - 1], q6_s)
        got(inv_s.at[0:88], a_s)

    def slot(t, carry):
        @pl.when(t + 2 < C)
        def _():
            forward_x(t + 2)

        @pl.when(t + 3 < C)
        def _():
            first_sends(t + 3)

        @pl.when(t + 1 < C)
        def _():
            forward_z(t + 1)

        @pl.when(t < C)
        def _():
            grads(t)

        @pl.when(t == SPLIT)
        def _():
            tail_out(0, SPLIT)

        for late, work in ((1, along_z_lo), (2, along_x)):

            @pl.when(t >= late)
            def _():
                work(t - late)

        for at, steps in ((3, ((start_y, 0),)), (4, ((along_y, 0),)), (5, ((along_z_hi_first, 0), (start_y, 1)))):

            @pl.when(t == at)
            def _():
                for work, g in steps:
                    work(g)

        return carry

    lax.fori_loop(0, C, slot, 0)
    gain_core()
    tail_out(SPLIT, C)
    along_x(C - 2)
    start_y(2)
    along_y(1)
    along_z_hi(0)
    last_z()
    gain_z_lo()
    tail_rows()
    along_z_hi_first(1)
    along_y(2)
    drain_first()
    back_y(0)
    last_x()
    gain_x()
    along_z_hi(1)
    along_z_hi_first(2)
    last_y()
    gain_y()
    gather_core(0)
    along_z_hi(2)
    back_y(1)
    last_z_hi()
    gain_z_hi()
    back_y(2)
    gather_core(1)
    gain_last()
    gather_core(2)
    last_back()
    drain_last()
    last_take()
    place = {}
    for core in range(2):
        for c in range(C):
            for qs in range(8):
                place[hidden_block(core, c, qs)] = (core, c, qs)
    for block in range(H // 128):
        pieces = []
        for i in range(per):
            core, c, qs = place[per * block + i]
            start = qs // per * 128
            pieces.append((go[core, c, :, start : start + 128], qs % per))
        o_g1[:, 128 * block : 128 * (block + 1)] = gather_lanes(pieces)


def place_kernel(*refs):
    count = len(refs) // 2
    for i in range(count):
        refs[count + i][...] = refs[i][...]


def body(tokens, cotangent, live_index, live_count, norm_gain, w_first, w_second):
    images, patches, width = tokens.shape
    tok, cot = tokens.reshape(ROWS, D), cotangent.reshape(ROWS, D)
    vmem = pl.BlockSpec(memory_space=pltpu.VMEM)
    smem = pl.BlockSpec(memory_space=pltpu.SMEM)
    dma = pltpu.SemaphoreType.DMA
    scratch = [
        pltpu.VMEM((2, C, R1 // 2, CW), BF16),
        pltpu.VMEM((C, 2, NX, SR, CW), BF16),
        pltpu.VMEM((2 * ROWS, D), BF16),
        pltpu.VMEM((2 * ROWS, D), BF16),
        pltpu.VMEM((2 * ROWS, D), BF16),
        pltpu.VMEM((D, 2 * ROWS), BF16),
        pltpu.VMEM((2 * ROWS, D), F32),
        pltpu.VMEM((2 * ROWS, 128), F32),
        pltpu.VMEM((ROWS, 128), F32),
        pltpu.VMEM((C, 2 * ROWS, CW), BF16),
        pltpu.VMEM((C, 2 * ROWS, CW), BF16),
        pltpu.VMEM((C, 2, NX, SR, CW), BF16),
        pltpu.VMEM((C, NX, SR, CW), BF16),
        pltpu.VMEM((C, NX, SR, CW), BF16),
        pltpu.VMEM((C, NX - 1, SR, CW), BF16),
        pltpu.VMEM((C, SR, CW), BF16),
        pltpu.VMEM((NY - 1, C, PR, CW), BF16),
        pltpu.VMEM((NZH, C, PR, CW), BF16),
        pltpu.VMEM((NY, C, PR, CW), BF16),
        pltpu.VMEM((C, PR, CW), BF16),
        pltpu.VMEM((NX, SR, CW), BF16),
        pltpu.VMEM((NX, SR, CW), BF16),
        pltpu.VMEM((2, NX, SR, CW), BF16),
        pltpu.VMEM((NX - 1, 2, SR, CW), BF16),
        pltpu.VMEM((2, SR, CW), BF16),
        pltpu.VMEM((NY - 1, 2, PR, CW), BF16),
        pltpu.VMEM((NZH, 2, PR, CW), BF16),
        pltpu.VMEM((NY, 2, PR, CW), BF16),
        pltpu.VMEM((2, 2, PR, CW), BF16),
        pltpu.VMEM((2, C, R1 // 2, CW), F32),
        pltpu.VMEM((2 * ROWS, D), F32),
        pltpu.VMEM((2 * ROWS, D), F32),
        pltpu.VMEM((2, ROWS, D), BF16),
        pltpu.VMEM((2, ROWS, D), BF16),
        pltpu.VMEM((2, NX, 8, 128), F32),
        pltpu.VMEM((4, 8, 128), F32),
        pltpu.VMEM((8, D), F32),
        pltpu.VMEM((4, 8, 128), F32),
        pltpu.VMEM((4, 8, 128), F32),
        pltpu.VMEM((4, 8, 128), F32),
        pltpu.VMEM((4, 8, 128), F32),
        dma, dma((C,)),
        dma, dma((C,)),
        dma, dma((C,)),
        dma, dma((C,)),
        dma, dma((C,)),
        dma, dma((3,)),
        dma, dma((3, 2)),
        dma, dma((3,)),
        dma, dma((3,)),
        dma, dma, dma,
        dma, dma, dma, dma, dma, dma, dma, dma, dma, dma,
        dma, dma,
        dma, dma,
        dma, dma((5,)),
        dma, dma,
        dma, dma((11,)),
    ]
    out, grad, g1, g2, gg = pl.pallas_call(
        kernel,
        out_shape=(
            jax.ShapeDtypeStruct((ROWS, D), BF16),
            jax.ShapeDtypeStruct((ROWS, D), BF16),
            jax.ShapeDtypeStruct((48, H), F32),
            jax.ShapeDtypeStruct((192, D), F32),
            jax.ShapeDtypeStruct((1, 48), F32),
        ),
        in_specs=[vmem, vmem, vmem, smem, vmem, vmem, vmem],
        out_specs=(vmem,) * 5,
        scratch_shapes=scratch,
        compiler_params=pltpu.CompilerParams(
            collective_id=0, has_side_effects=True, vmem_limit_bytes=60 << 20
        ),
        cost_estimate=pl.CostEstimate(flops=14 * 10**9, bytes_accessed=10**7, transcendentals=0),
    )(tok, cot, live_index, live_count, norm_gain.reshape(1, 48), w_first, w_second)
    made = (out, grad, g1, g2, gg)
    out, grad, g1, g2, gg = pl.pallas_call(
        place_kernel,
        out_shape=tuple(jax.ShapeDtypeStruct(v.shape, v.dtype) for v in made),
        in_specs=[vmem] * 5,
        out_specs=(vmem,) * 5,
    )(*made)
    return (
        out.reshape(images, patches, width),
        grad.reshape(images, patches, width),
        g1,
        g2,
        gg.reshape(48),
    )


def solution(mesh):
    return jax.shard_map(
        body,
        mesh=mesh,
        in_specs=(
            P(("dp", "fsdp"), None, None),
            P(("dp", "fsdp"), None, None),
            P(("dp", "fsdp"), None),
            P(("dp", "fsdp")),
            P("fsdp"),
            P("fsdp", None),
            P("fsdp", None),
        ),
        out_specs=(
            P(("dp", "fsdp"), None, None),
            P(("dp", "fsdp"), None, None),
            P("fsdp", None),
            P("fsdp", None),
            P("fsdp"),
        ),
        check_vma=False,
    )
```

```python
import functools

import jax
import jax.numpy as jnp
from jax import lax
from jax.experimental import pallas as pl
from jax.experimental.pallas import tpu as pltpu
from jax.sharding import PartitionSpec as P

epsilon = 1e-06
root_two_pi = 0.7978845608028654
cubic = 0.044715

MESH = pl.DeviceIdType.MESH
NX, NY, NZH = 4, 4, 4
D, H, ROWS, PATCHES = 768, 3072, 512, 256
SPLIT = 4
GROUPS = ((0, 2), (2, 4), (4, 5))
C = 6
HS = 192 // C
CW = 8 * HS
R1, R2 = D // 8, D * HS // CW
NB = D // CW
SR = R1 + R2
PR = SR // NY
SCALE = 1.0 / PATCHES
F32, BF16 = jnp.float32, jnp.bfloat16


def rem(a, n):
    return lax.rem(a, jnp.int32(n))


def kernel(tok, cot, idx, cnt, gain, w_in, w2, o_out, o_grad, o_g1, o_g2, o_gain,
           w1, wg, tk, ct, nrm, nt, nf, inv_s, flag_s, hid, bb, buf, r1, s1, r2, s2, r3, r4, fin, gx,
           e1, eb, sl1, rl2, sl2, rl3, rl4, finl, xg, go, po, pb, px, rx, gt, gsum, gacc, gz, gxx, gyy, gzz,
           ag_s, ag_r, az_s, az_r, ay_s, ay_r, q1_s, q1_r, q2_s, q2_r, q3_s, q3_r, q4_s, q4_r, q5_s, q5_r, q6_s, q6_r,
           qe_r, qb_s, qb_r, l2_s, l2_r, l3_s, l3_r, l4_s, l4_r, l5_s, l5_r, l6_s, l6_r,
           w_s, w_r, t_s, t_r, gg_s, gg_r, p_s, p_r, a_s, a_r):
    dp, f = lax.axis_index("dp"), lax.axis_index("fsdp")
    x, zl, k = lax.div(f, jnp.int32(4)), rem(lax.div(f, jnp.int32(2)), 2), rem(f, 2)
    zh, y = lax.div(dp, jnp.int32(4)), rem(dp, 4)
    z, q = zh * 2 + zl, lax.div(f, jnp.int32(2))

    def dev(x_, y_, z_, k_):
        return (lax.div(z_, jnp.int32(2)) * 4 + y_, x_ * 4 + rem(z_, 2) * 2 + k_)

    z_near = zh * 2 + (1 - zl)
    z_far = rem(z + 8 + 2 * zl - 1, 8)
    partner = dev(x, y, z, 1 - k)
    near, far = dev(x, y, z_near, k), dev(x, y, z_far, k)
    xp = [dev(rem(x + i, NX), y, z, k) for i in range(1, NX)]
    yp = [dev(x, rem(y + i, NY), z, k) for i in range(1, NY)]
    zp = [dev(x, y, rem(z + 2 * i, 8), k) for i in range(1, NZH)]

    def send(src, dst, s_sem, r_sem, to):
        copy = pltpu.make_async_remote_copy(
            src_ref=src, dst_ref=dst, send_sem=s_sem, recv_sem=r_sem, device_id=to, device_id_type=MESH
        )
        copy.start()

    def got(ref, sem):
        pltpu.make_async_copy(ref, ref, sem).wait()

    near_other, far_other = dev(x, y, z_near, 1 - k), dev(x, y, z_far, 1 - k)
    everyone = [partner, near, far, near_other, far_other] + xp + yp + zp
    barrier = pltpu.get_barrier_semaphore()
    for peer in everyone:
        pl.semaphore_signal(barrier, inc=1, device_id=peer, device_id_type=MESH)

    lane = lax.broadcasted_iota(jnp.int32, (R1 // 2, 128), 1)
    per = 128 // HS

    def gather_lanes(pieces):
        block = None
        for i, (value, at) in enumerate(pieces):
            turned = value if at == i else pltpu.roll(value, (i - at) * HS % 128, 1)
            block = turned if block is None else jnp.where(lane >= HS * i, turned, block)
        return block

    def hidden_block(core, c, qs):
        return (2 * qs + core) * C + c

    gains_own = jnp.broadcast_to(gain[...].astype(F32), (8, 48))
    gsum[0] = jnp.zeros((8, 128), F32)
    for core in range(2):

        @pl.when(k == core)
        def _():
            gsum[0, :, 48 * core : 48 * (core + 1)] = gains_own

    gacc[...] = jnp.zeros((8, D), F32)
    y_odd = rem(y, 2) == 1

    @pl.when(jnp.logical_not(y_odd))
    def _():
        for core in range(2):
            for c in range(C):
                for part in range(CW // 128):
                    pieces = []
                    for i in range(per):
                        block = hidden_block(core, c, per * part + i)
                        start = block // per * 128
                        pieces.append((w_in[:, start : start + 128].astype(F32), block % per))
                    w1[core, c, :, 128 * part : 128 * (part + 1)] = gather_lanes(pieces).astype(BF16)

    @pl.when(y_odd)
    def _():
        for c in range(C):
            for n in range(NB):
                wg[c, zl, x, R1 + HS * n : R1 + HS * (n + 1), :] = w2[
                    HS * c : HS * (c + 1), CW * n : CW * (n + 1)
                ]

    pl.semaphore_wait(barrier, len(everyone))

    send(gsum.at[0], gsum.at[1], gg_s, gg_r.at[0], partner)
    mine = pl.ds(pl.multiple_of(R1 // 2 * k, 16), R1 // 2)
    other = pl.ds(pl.multiple_of(R1 // 2 * (1 - k), 16), R1 // 2)

    @pl.when(jnp.logical_not(y_odd))
    def _():
        send(w1.at[1 - k], wg.at[:, zl, x, mine, :], w_s, w_r, partner)
        for c in range(C):
            wg[c, zl, x, mine, :] = w1[k, c]
        got(wg.at[:, zl, x, other, :], w_r)

    half = rem(y, 2)
    my_half = pl.ds(pl.multiple_of(SR // 2 * half, 16), SR // 2)
    its_half = pl.ds(pl.multiple_of(SR // 2 * (1 - half), 16), SR // 2)

    def pick(cond, a, b):
        return tuple(jnp.where(cond, i, j) for i, j in zip(a, b))

    def first_sends(c):
        block = wg.at[c, zl, x, my_half]
        for i in range(1, NX):
            send(block, block, ag_s, ag_r.at[c], xp[i - 1])

    first_sends(0)

    got(gsum.at[1], gg_r.at[0])
    gt[zl, x] = gsum[0] + gsum[1]
    for i in range(1, NX):
        send(gt.at[zl, x], gt.at[zl, x], gg_s, gg_r.at[i], xp[i - 1])

    for image in range(2):
        at = lax.broadcasted_iota(jnp.int32, (PATCHES, PATCHES), 0)
        place = lax.broadcasted_iota(jnp.int32, (PATCHES, PATCHES), 1)
        hit = jnp.where(
            jnp.logical_and(idx[image : image + 1, :] == at, place < cnt[image]), 1.0, 0.0
        ).astype(F32)
        flag = jnp.max(hit, axis=1, keepdims=True)
        rows = slice(PATCHES * image, PATCHES * (image + 1))
        flag_s[rows, :] = jnp.broadcast_to(flag, (PATCHES, 128))
        to = pl.ds(pl.multiple_of(ROWS * k + PATCHES * image, PATCHES), PATCHES)
        tk[to, :] = jnp.where(flag > 0, tok[rows, :].astype(F32), 0.0).astype(BF16)
        ct[to, :] = jnp.where(flag > 0, cot[rows, :].astype(F32), 0.0).astype(BF16)
    here = pl.ds(pl.multiple_of(ROWS * k, ROWS), ROWS)
    there = pl.ds(pl.multiple_of(ROWS * (1 - k), ROWS), ROWS)
    send(tk.at[here], tk.at[here], t_s, t_r, partner)
    send(ct.at[here], ct.at[here], t_s, t_r, partner)

    def swap(c, kind, spread, to):
        if spread:
            for i, ends in enumerate((yp[0], yp[2])):
                block = wg.at[c, kind, 2 * i : 2 * i + 2, my_half]
                send(block, block, ay_s, ay_r.at[c], ends)
        else:
            block = wg.at[c, kind, :, my_half]
            send(block, block, ay_s, ay_r.at[c], to)

    def forward_x(c, spread=True):
        got(wg.at[c, zl, 0 : NX - 1, my_half], ag_r.at[c])
        for i, to in enumerate((near, far)):
            block = wg.at[c, zl, 2 * i : 2 * i + 2, my_half]
            send(block, block, az_s, az_r.at[c], to)
        swap(c, zl, spread, yp[0])

    def forward_z(c, spread=True):
        got(wg.at[c, 1 - zl, :, my_half], az_r.at[c])
        swap(c, 1 - zl, spread, yp[2])

    for i in range(1, NX):
        got(gt.at[zl, rem(x + NX - i, NX)], gg_r.at[i])
    send(gt.at[zl], gt.at[zl], gg_s, gg_r.at[4], near)
    forward_x(0, spread=True)
    first_sends(1)
    got(gt.at[1 - zl], gg_r.at[4])
    got(tk, t_r)

    def gain_row():
        total = jnp.zeros((8, D), F32)
        for qs in range(8):
            tile = jnp.concatenate([gt[qs % 2, qs // 2], jnp.zeros((8, D - 128), F32)], axis=1)
            total = total + (pltpu.roll(tile, 96 * qs, 1) if qs else tile)
        return total[0:1, :]

    gains = gain_row()

    def norm_step(m, carry):
        rows = pl.ds(pl.multiple_of(256 * m, 256), 256)
        values = tk[rows, :].astype(F32)
        center = jnp.mean(values, axis=1, keepdims=True)
        values = values - center
        spread = jnp.mean(values * values, axis=1, keepdims=True)
        inverse = lax.rsqrt(spread + epsilon)
        normed = values * inverse
        nf[rows, :] = normed
        inv_s[rows, :] = jnp.broadcast_to(inverse, (256, 128))
        normal = normed * gains
        nrm[rows, :] = normal.astype(BF16)
        nt[:, rows] = jnp.transpose(normal).astype(BF16)
        return carry

    lax.fori_loop(0, 4, norm_step, 0)
    forward_z(0, spread=True)
    forward_x(1)
    first_sends(2)

    def first_of(c):
        return jnp.concatenate([wg[c, qs % 2, qs // 2, 0:R1, :] for qs in range(8)], axis=0)

    def second_of(c, n):
        rows = slice(R1 + HS * n, R1 + HS * (n + 1))
        return jnp.concatenate([wg[c, qs % 2, qs // 2, rows, :] for qs in range(8)], axis=0)

    def grads(c):
        got(wg.at[c, :, :, its_half], ay_r.at[c])

        def step(m, carry):
            rows = pl.ds(pl.multiple_of(256 * m, 256), 256)
            before = jnp.dot(nrm[rows, :], first_of(c), preferred_element_type=F32)
            back = jnp.zeros((256, CW), F32)
            for n in range(NB):
                back = back + lax.dot_general(
                    ct[rows, CW * n : CW * (n + 1)], second_of(c, n), (((1,), (1,)), ((), ())),
                    preferred_element_type=F32,
                )
            square = before * before
            tangent = jnp.tanh(before * (root_two_pi + (root_two_pi * cubic) * square))
            half = 0.5 + 0.5 * tangent
            hid[c, rows, :] = (before * half).astype(BF16)
            slope = half + (0.5 * before) * (1.0 - tangent * tangent) * (
                root_two_pi + (3.0 * cubic * root_two_pi) * square
            )
            bb[c, rows, :] = (back * slope).astype(BF16)
            return carry

        lax.fori_loop(0, 4, step, 0, unroll=True)
        for part in range(2):
            term = jnp.dot(nt[384 * part : 384 * (part + 1), :], bb[c], preferred_element_type=F32)
            own_rows = jnp.concatenate(
                [wg[c, qs % 2, qs // 2, 0:R1, :] for qs in range(4 * part, 4 * part + 4)], axis=0
            )
            product = term * own_rows.astype(F32)
            high = product.astype(BF16)
            low = (product - high.astype(F32)).astype(BF16)
            ones = jnp.ones((8, CW), BF16)
            line_sum = jnp.zeros((8, 384), F32)
            for share in (high, low):
                line_sum = line_sum + lax.dot_general(
                    ones, share, (((1,), (1,)), ((), ())), preferred_element_type=F32
                )
            gacc[:, 384 * part : 384 * (part + 1)] += line_sum
            term = (term * SCALE).astype(BF16)
            for i in range(4):
                qs = 4 * part + i
                buf[c, qs % 2, qs // 2, 0:R1, :] = term[R1 * i : R1 * (i + 1), :]
        for n in range(NB):
            term = lax.dot_general(
                hid[c], ct[:, CW * n : CW * (n + 1)], (((0,), (0,)), ((), ())), preferred_element_type=F32
            )
            term = (term * SCALE).astype(BF16)
            for qs in range(8):
                buf[c, qs % 2, qs // 2, R1 + HS * n : R1 + HS * (n + 1), :] = term[HS * qs : HS * (qs + 1), :]
        to_odd = jnp.logical_and(c == C - 1, k == 0)

        @pl.when(jnp.logical_not(to_odd))
        def _():
            send(buf.at[c, 1 - zl, 0:2], r1.at[c, 0:2], q1_s, q1_r.at[c], near)
            send(buf.at[c, 1 - zl, 2:4], r1.at[c, 2:4], q1_s, q1_r.at[c], far)

        @pl.when(to_odd)
        def _():
            send(buf.at[c, 1 - zl, 0:2], e1.at[0:2], q1_s, qe_r, near_other)
            send(buf.at[c, 1 - zl, 2:4], e1.at[2:4], q1_s, qe_r, far_other)
            send(buf.at[c, zl], eb, qb_s, qb_r, partner)

    def along_z_lo(c):
        got(r1.at[c], q1_r.at[c])
        for i in range(NX):
            s1[c, i] = (buf[c, zl, i].astype(F32) + r1[c, i].astype(F32)).astype(BF16)
        for i in range(1, NX):
            send(s1.at[c, rem(x + i, NX)], r2.at[c, i - 1], q2_s, q2_r.at[c], xp[i - 1])

    def along_x(c):
        got(r2.at[c], q2_r.at[c])
        total = s1[c, x].astype(F32)
        for i in range(NX - 1):
            total = total + r2[c, i].astype(F32)
        s2[c] = total.astype(BF16)

    def start_y(g):
        first, end = GROUPS[g]
        for i in range(1, NY):
            part = pl.ds(pl.multiple_of(PR * rem(y + i, NY), 16), PR)
            send(s2.at[first:end, part], r3.at[i - 1, first:end], q3_s, q3_r.at[g], yp[i - 1])

    def along_y(g):
        first, end = GROUPS[g]
        got(r3.at[:, first:end], q3_r.at[g])
        total = s2[first:end, pl.ds(pl.multiple_of(PR * y, 16), PR), :].astype(F32)
        for i in range(NY - 1):
            total = total + r3[i, first:end].astype(F32)
        r4[0, first:end] = total.astype(BF16)
        to = pick(jnp.logical_xor(rem(zh, 2) == 0, g % 2 == 0), zp[2], zp[0])
        send(r4.at[0, first:end], r4.at[1, first:end], q4_s, q4_r.at[g, 0], to)

    def spread_y(g, total):
        first, end = GROUPS[g]
        fin[y, first:end] = total.astype(BF16)
        for i in range(1, NY):
            send(fin.at[y, first:end], fin.at[y, first:end], q5_s, q5_r.at[g], yp[i - 1])

    def along_z_hi_first(g):
        first, end = GROUPS[g]
        got(r4.at[1, first:end], q4_r.at[g, 0])
        r4[2, first:end] = (r4[0, first:end].astype(F32) + r4[1, first:end].astype(F32)).astype(BF16)
        to = pick(jnp.logical_xor(rem(zh, 2) == 0, g % 2 == 0), zp[0], zp[2])
        send(r4.at[2, first:end], r4.at[3, first:end], q4_s, q4_r.at[g, 1], to)

    def along_z_hi(g):
        first, end = GROUPS[g]
        got(r4.at[3, first:end], q4_r.at[g, 1])
        spread_y(g, r4[2, first:end].astype(F32) + r4[3, first:end].astype(F32))

    def put_second(c, parts):
        second = parts.reshape(R2, CW).astype(F32)
        for n in range(NB):
            o_g2[HS * c : HS * (c + 1), CW * n : CW * (n + 1)] = second[HS * n : HS * (n + 1), :]

    def back_y(g):
        first, end = GROUPS[g]
        got(fin.at[0 : NY - 1, first:end], q5_r.at[g])
        send(fin.at[1 - k, first:end], gx.at[first:end], q6_s, q6_r.at[g], partner)
        go[k, first:end] = fin[k, first:end].astype(F32)
        for c in range(first, end):
            put_second(c, fin[2:4, c])

    def gather_core(g):
        first, end = GROUPS[g]
        got(gx.at[first:end], q6_r.at[g])
        go[1 - k, first:end] = gx[first:end].astype(F32)

    def last_z():
        @pl.when(k == 1)
        def _():
            got(eb, qb_r)
            got(r1.at[C - 1], q1_r.at[C - 1])
            got(e1, qe_r)
            for i in range(NX):
                sl1[0, i] = (eb[i].astype(F32) + e1[i].astype(F32)).astype(BF16)
                sl1[1, i] = (buf[C - 1, zl, i].astype(F32) + r1[C - 1, i].astype(F32)).astype(BF16)
            for i in range(1, NX):
                send(sl1.at[:, rem(x + i, NX)], rl2.at[i - 1], l2_s, l2_r, xp[i - 1])

    def last_x():
        @pl.when(k == 1)
        def _():
            got(rl2, l2_r)
            total = sl1[:, x].astype(F32)
            for i in range(NX - 1):
                total = total + rl2[i].astype(F32)
            sl2[...] = total.astype(BF16)
            for i in range(1, NY):
                part = pl.ds(pl.multiple_of(PR * rem(y + i, NY), 16), PR)
                send(sl2.at[:, part], rl3.at[i - 1], l3_s, l3_r, yp[i - 1])

    def last_y():
        @pl.when(k == 1)
        def _():
            got(rl3, l3_r)
            total = sl2[:, pl.ds(pl.multiple_of(PR * y, 16), PR), :].astype(F32)
            for i in range(NY - 1):
                total = total + rl3[i].astype(F32)
            rl4[zh] = total.astype(BF16)
            for i in range(1, NZH):
                send(rl4.at[zh], rl4.at[zh], l4_s, l4_r, zp[i - 1])

    def last_z_hi():
        @pl.when(k == 1)
        def _():
            got(rl4.at[0 : NZH - 1], l4_r)
            total = rl4[0].astype(F32)
            for i in range(1, NZH):
                total = total + rl4[i].astype(F32)
            finl[y] = total.astype(BF16)
            for i in range(1, NY):
                send(finl.at[y], finl.at[y], l5_s, l5_r, yp[i - 1])

    def last_back():
        @pl.when(k == 1)
        def _():
            got(finl.at[0 : NY - 1], l5_r)
            send(finl.at[0], xg.at[0], l6_s, l6_r, partner)
            send(finl.at[2:4, 0], xg.at[1], l6_s, l6_r, partner)
            go[:, C - 1] = finl[1].astype(F32)
            put_second(C - 1, finl[2:4, 1])

    def last_take():
        @pl.when(k == 0)
        def _():
            got(xg, l6_r)
            go[:, C - 1] = xg[0].astype(F32)
            put_second(C - 1, xg[1])
            got(eb, qb_s)

        @pl.when(k == 1)
        def _():
            got(rl2, l2_s)
            got(rl3, l3_s)
            got(rl4.at[0 : NZH - 1], l4_s)
            got(finl.at[0 : NY - 1], l5_s)
            got(xg, l6_s)

    def out_rows(start, first, end):
        rows = pl.ds(pl.multiple_of(start, 256), 256)
        parts = []
        for n in range(NB):
            total = jnp.zeros((256, CW), F32)
            for c in range(first, end):
                total = total + jnp.dot(hid[c, rows, :], second_of(c, n), preferred_element_type=F32)
            parts.append(total)
        return jnp.concatenate(parts, axis=1)

    def back_rows(start, first, end):
        rows = pl.ds(pl.multiple_of(start, 256), 256)
        total = jnp.zeros((256, D), F32)
        for c in range(first, end):
            total = total + lax.dot_general(
                bb[c, rows, :], first_of(c), (((1,), (1,)), ((), ())), preferred_element_type=F32
            )
        return total

    def tail_out(first, end):
        def step(m, carry):
            m = lax.rem(m + 2 * (1 - k), 4)
            rows = pl.ds(pl.multiple_of(256 * m, 256), 256)
            mixed, back = out_rows(256 * m, first, end), back_rows(256 * m, first, end)
            if first > 0:
                mixed, back = mixed + po[rows, :], back + pb[rows, :]
            po[rows, :] = mixed
            pb[rows, :] = back
            return carry

        if first == 0:
            lax.fori_loop(0, 4, step, 0, unroll=True)
            return
        lax.fori_loop(0, 2, step, 0, unroll=True)
        px[0] = po[there, :].astype(BF16)
        px[1] = pb[there, :].astype(BF16)
        for i in range(2):
            send(px.at[i], rx.at[i], p_s, p_r, partner)
        lax.fori_loop(2, 4, step, 0, unroll=True)

    def tail_rows():
        got(rx, p_r)

        def step(m, carry):
            rows = pl.ds(pl.multiple_of(128 * m, 128), 128)
            at = pl.ds(pl.multiple_of(ROWS * k + 128 * m, 128), 128)
            live = flag_s[rows, :][:, 0:1] > 0
            plain = tok[rows, :].astype(F32)
            mixed = plain + (po[at, :] + rx[0, rows, :].astype(F32))
            o_out[rows, :] = jnp.where(live, mixed, plain).astype(BF16)
            normed = nf[at, :]
            inverse = inv_s[at, :][:, 0:1]
            back = pb[at, :] + rx[1, rows, :].astype(F32)
            scaled = back * gains
            first = jnp.mean(scaled, axis=1, keepdims=True)
            second = jnp.mean(scaled * normed, axis=1, keepdims=True)
            upstream = cot[rows, :].astype(F32)
            value = upstream + inverse * (scaled - first - normed * second)
            o_grad[rows, :] = jnp.where(live, value, upstream).astype(BF16)
            return carry

        lax.fori_loop(0, 4, step, 0)

    def gain_core():
        row = gacc[...] * SCALE / gains
        tile = jnp.zeros((8, 128), F32)
        line = lax.broadcasted_iota(jnp.int32, (8, 128), 0)
        for qs in range(8):
            turned = (pltpu.roll(row, D - 96 * qs, 1) if qs else row)[:, 0:128]
            tile = jnp.where(line == qs, turned, tile)
        gz[0] = tile
        send(gz.at[0], gz.at[1], a_s, a_r.at[0], partner)

    def gain_z_lo():
        got(gz.at[1], a_r.at[0])
        gz[2] = gz[0] + gz[1]
        send(gz.at[2], gz.at[3], a_s, a_r.at[1], near)

    def gain_x():
        got(gz.at[3], a_r.at[1])
        gxx[x] = gz[2] + gz[3]
        for i in range(1, NX):
            send(gxx.at[x], gxx.at[x], a_s, a_r.at[1 + i], xp[i - 1])

    def gain_y():
        for i in range(1, NX):
            got(gxx.at[rem(x + NX - i, NX)], a_r.at[1 + i])
        gyy[y] = gxx[0] + gxx[1] + gxx[2] + gxx[3]
        for i in range(1, NY):
            send(gyy.at[y], gyy.at[y], a_s, a_r.at[4 + i], yp[i - 1])

    def gain_z_hi():
        for i in range(1, NY):
            got(gyy.at[rem(y + NY - i, NY)], a_r.at[4 + i])
        gzz[zh] = gyy[0] + gyy[1] + gyy[2] + gyy[3]
        for i in range(1, NZH):
            send(gzz.at[zh], gzz.at[zh], a_s, a_r.at[7 + i], zp[i - 1])

    def gain_last():
        for i in range(1, NZH):
            got(gzz.at[rem(zh + NZH - i, NZH)], a_r.at[7 + i])
        total = gzz[0] + gzz[1] + gzz[2] + gzz[3]
        line = lax.broadcasted_iota(jnp.int32, (8, 128), 0)
        row = jnp.sum(jnp.where(line == q, total, 0.0), axis=0, keepdims=True)
        row = jnp.broadcast_to(row, (8, 128))
        row = jnp.where(k == 1, pltpu.roll(row, 80, 1), row)
        o_gain[...] = row[0:1, 0:48]

    def drain_first():
        got(r2.at[:, :, 0 : SR // 2], ag_s)
        got(wg.at[:, 0, :, 0 : SR // 2], az_s)
        got(wg.at[:, :, :, 0 : SR // 2], ay_s)
        got(r1, q1_s)
        got(tk, t_s)
        got(px, p_s)
        got(inv_s.at[0:64], gg_s)

        @pl.when(jnp.logical_not(y_odd))
        def _():
            got(wg.at[:, zl, x, mine, :], w_s)

    def drain_last():
        got(r2.at[0 : C - 1], q2_s)
        got(r3.at[:, 0 : C - 1], q3_s)
        got(r4.at[0:2, 0 : C - 1], q4_s)
        got(fin.at[0 : NY - 1, 0 : C - 1], q5_s)
        got(gx.at[0 : C - 1], q6_s)
        got(inv_s.at[0:88], a_s)

    def slot(t, carry):
        @pl.when(t + 1 < C)
        def _():
            forward_z(t + 1)

        @pl.when(t + 2 < C)
        def _():
            forward_x(t + 2)

        @pl.when(t + 3 < C)
        def _():
            first_sends(t + 3)

        @pl.when(t < C)
        def _():
            grads(t)

        @pl.when(t == SPLIT)
        def _():
            tail_out(0, SPLIT)

        for late, work in ((1, along_z_lo), (2, along_x)):

            @pl.when(t >= late)
            def _():
                work(t - late)

        for at, steps in ((3, ((start_y, 0),)), (4, ((along_y, 0),)), (5, ((along_z_hi_first, 0), (start_y, 1)))):

            @pl.when(t == at)
            def _():
                for work, g in steps:
                    work(g)

        return carry

    lax.fori_loop(0, C, slot, 0)
    gain_core()
    tail_out(SPLIT, C)
    along_x(C - 2)
    start_y(2)
    along_y(1)
    along_z_hi(0)
    last_z()
    gain_z_lo()
    tail_rows()
    along_z_hi_first(1)
    along_y(2)
    drain_first()
    back_y(0)
    last_x()
    gain_x()
    along_z_hi(1)
    along_z_hi_first(2)
    last_y()
    gain_y()
    gather_core(0)
    along_z_hi(2)
    back_y(1)
    last_z_hi()
    gain_z_hi()
    back_y(2)
    gather_core(1)
    gain_last()
    gather_core(2)
    last_back()
    drain_last()
    last_take()
    place = {}
    for core in range(2):
        for c in range(C):
            for qs in range(8):
                place[hidden_block(core, c, qs)] = (core, c, qs)
    for block in range(H // 128):
        pieces = []
        for i in range(per):
            core, c, qs = place[per * block + i]
            start = qs // per * 128
            pieces.append((go[core, c, :, start : start + 128], qs % per))
        o_g1[:, 128 * block : 128 * (block + 1)] = gather_lanes(pieces)


def place_kernel(*refs):
    count = len(refs) // 2
    for i in range(count):
        refs[count + i][...] = refs[i][...]


def body(tokens, cotangent, live_index, live_count, norm_gain, w_first, w_second):
    images, patches, width = tokens.shape
    tok, cot = tokens.reshape(ROWS, D), cotangent.reshape(ROWS, D)
    vmem = pl.BlockSpec(memory_space=pltpu.VMEM)
    smem = pl.BlockSpec(memory_space=pltpu.SMEM)
    dma = pltpu.SemaphoreType.DMA
    scratch = [
        pltpu.VMEM((2, C, R1 // 2, CW), BF16),
        pltpu.VMEM((C, 2, NX, SR, CW), BF16),
        pltpu.VMEM((2 * ROWS, D), BF16),
        pltpu.VMEM((2 * ROWS, D), BF16),
        pltpu.VMEM((2 * ROWS, D), BF16),
        pltpu.VMEM((D, 2 * ROWS), BF16),
        pltpu.VMEM((2 * ROWS, D), F32),
        pltpu.VMEM((2 * ROWS, 128), F32),
        pltpu.VMEM((ROWS, 128), F32),
        pltpu.VMEM((C, 2 * ROWS, CW), BF16),
        pltpu.VMEM((C, 2 * ROWS, CW), BF16),
        pltpu.VMEM((C, 2, NX, SR, CW), BF16),
        pltpu.VMEM((C, NX, SR, CW), BF16),
        pltpu.VMEM((C, NX, SR, CW), BF16),
        pltpu.VMEM((C, NX - 1, SR, CW), BF16),
        pltpu.VMEM((C, SR, CW), BF16),
        pltpu.VMEM((NY - 1, C, PR, CW), BF16),
        pltpu.VMEM((NZH, C, PR, CW), BF16),
        pltpu.VMEM((NY, C, PR, CW), BF16),
        pltpu.VMEM((C, PR, CW), BF16),
        pltpu.VMEM((NX, SR, CW), BF16),
        pltpu.VMEM((NX, SR, CW), BF16),
        pltpu.VMEM((2, NX, SR, CW), BF16),
        pltpu.VMEM((NX - 1, 2, SR, CW), BF16),
        pltpu.VMEM((2, SR, CW), BF16),
        pltpu.VMEM((NY - 1, 2, PR, CW), BF16),
        pltpu.VMEM((NZH, 2, PR, CW), BF16),
        pltpu.VMEM((NY, 2, PR, CW), BF16),
        pltpu.VMEM((2, 2, PR, CW), BF16),
        pltpu.VMEM((2, C, R1 // 2, CW), F32),
        pltpu.VMEM((2 * ROWS, D), F32),
        pltpu.VMEM((2 * ROWS, D), F32),
        pltpu.VMEM((2, ROWS, D), BF16),
        pltpu.VMEM((2, ROWS, D), BF16),
        pltpu.VMEM((2, NX, 8, 128), F32),
        pltpu.VMEM((4, 8, 128), F32),
        pltpu.VMEM((8, D), F32),
        pltpu.VMEM((4, 8, 128), F32),
        pltpu.VMEM((4, 8, 128), F32),
        pltpu.VMEM((4, 8, 128), F32),
        pltpu.VMEM((4, 8, 128), F32),
        dma, dma((C,)),
        dma, dma((C,)),
        dma, dma((C,)),
        dma, dma((C,)),
        dma, dma((C,)),
        dma, dma((3,)),
        dma, dma((3, 2)),
        dma, dma((3,)),
        dma, dma((3,)),
        dma, dma, dma,
        dma, dma, dma, dma, dma, dma, dma, dma, dma, dma,
        dma, dma,
        dma, dma,
        dma, dma((5,)),
        dma, dma,
        dma, dma((11,)),
    ]
    out, grad, g1, g2, gg = pl.pallas_call(
        kernel,
        out_shape=(
            jax.ShapeDtypeStruct((ROWS, D), BF16),
            jax.ShapeDtypeStruct((ROWS, D), BF16),
            jax.ShapeDtypeStruct((48, H), F32),
            jax.ShapeDtypeStruct((192, D), F32),
            jax.ShapeDtypeStruct((1, 48), F32),
        ),
        in_specs=[vmem, vmem, vmem, smem, vmem, vmem, vmem],
        out_specs=(vmem,) * 5,
        scratch_shapes=scratch,
        compiler_params=pltpu.CompilerParams(
            collective_id=0, has_side_effects=True, vmem_limit_bytes=60 << 20
        ),
        cost_estimate=pl.CostEstimate(flops=14 * 10**9, bytes_accessed=10**7, transcendentals=0),
    )(tok, cot, live_index, live_count, norm_gain.reshape(1, 48), w_first, w_second)
    made = (out, grad, g1, g2, gg)
    out, grad, g1, g2, gg = pl.pallas_call(
        place_kernel,
        out_shape=tuple(jax.ShapeDtypeStruct(v.shape, v.dtype) for v in made),
        in_specs=[vmem] * 5,
        out_specs=(vmem,) * 5,
    )(*made)
    return (
        out.reshape(images, patches, width),
        grad.reshape(images, patches, width),
        g1,
        g2,
        gg.reshape(48),
    )


def solution(mesh):
    return jax.shard_map(
        body,
        mesh=mesh,
        in_specs=(
            P(("dp", "fsdp"), None, None),
            P(("dp", "fsdp"), None, None),
            P(("dp", "fsdp"), None),
            P(("dp", "fsdp")),
            P("fsdp"),
            P("fsdp", None),
            P("fsdp", None),
        ),
        out_specs=(
            P(("dp", "fsdp"), None, None),
            P(("dp", "fsdp"), None, None),
            P("fsdp", None),
            P("fsdp", None),
            P("fsdp"),
        ),
        check_vma=False,
    )
```
